128 devices in a mesh: row: 8 (over y, core), col: 16 (over z, x).
Axes of the slice: x: 4, y: 4, z: 4, core: 2. Of those that a mesh axis runs over, the one named last changes fastest.
Arguments:
- x_blocks: float32 [8, 64, 9, 128, 128], P('row', 'col'), may hold values from -1.2 to 1.2
- pattern: int32 [8, 64, 9], P('row', 'col'), may hold values 0 or 1
- alpha: float32 [], replicated, may hold values from 1 to 2
- beta: float32 [], replicated, may hold values from -1 to -0.5
Outputs:
- updated: float32 [8, 64, 9, 128, 128], P('row', 'col')
- trace: float32 [], replicated
The draws below stay inside these ranges and needn't reach their ends.
All inputs are finite; a program needn't handle non-finite values. No bound on the sum of `pattern` on one device may be relied on, other than what follows from the above.
Results may differ from the reference program's by a relative error of at most 0.0001.
Values sent between devices are 32-bit elements; how exact they have to be, the bound alone decides.
No kernel may reach another device: no remote copies, remote signals or barrier semaphores. Data moves between devices by JAX's collectives and lax.ppermute only.
A program may use at most 64 MiB of HBM per device.

```python
import jax
import jax.numpy as jnp
from jax import lax

B = 128
SLOTS = 9
NU = 8
NV = 64


def touch_ends(array, rng, least, top_value):
    longest = array.shape.index(max(array.shape))
    spots = []
    for shift in (0, 1):
        where = [jax.random.randint(jax.random.fold_in(rng, axis), (), 0, length) for axis, length in enumerate(array.shape)]
        where[longest] = (where[longest] + shift) % array.shape[longest]
        spots.append(tuple(where))
    return array.at[spots[0]].set(least).at[spots[1]].set(top_value)


def block_scale(stream_key, dims, cuts, low, high):
    loudness = 1.0
    for axis_at, parts in cuts:
        heights = jax.random.uniform(jax.random.fold_in(jax.random.fold_in(stream_key, 6), axis_at), (parts,), jnp.float32, low / len(cuts), high / len(cuts))
        loudness = loudness * jnp.repeat(jnp.exp(heights), dims[axis_at] // parts).reshape((-1,) + (1,) * (len(dims) - 1 - axis_at))
    return loudness


def scatter_about(own_key, shape, spread, bound, split=(), held_as=jnp.bfloat16):
    loudness = block_scale(own_key, shape, split, -0.22, 0.18) if split else 1.0
    drawn = jax.random.normal(own_key, shape, jnp.float32) * spread * loudness
    return jnp.minimum(jnp.maximum(drawn, -bound), bound).astype(held_as)


def setup_inputs(seed: int = 0) -> dict:
    streams_of = jax.random.split(jax.random.key(seed), 5)
    x_blocks = scatter_about(streams_of[0], (NU, NV, SLOTS, B, B), 0.2, 1.2, ((0, 8), (1, 16)), jnp.float32)
    pattern = touch_ends((jax.random.randint(streams_of[1], (NU, NV, SLOTS), 0, 3) < 2).astype(jnp.int32), jax.random.fold_in(streams_of[1], 1), 0, 1)
    alpha = jnp.clip(jax.random.uniform(streams_of[2], (), jnp.float32, 1.0, 2.0), 1.0, 2.0)
    beta = jnp.clip(jax.random.uniform(streams_of[3], (), jnp.float32, -1.0, -0.5), -1.0, -0.5)
    return dict(x_blocks=x_blocks, pattern=pattern, alpha=alpha, beta=beta)


STENCIL = [(-1, -1), (-1, 0), (-1, 1), (0, -1), (0, 0), (0, 1), (1, -1), (1, 0), (1, 1)]


def slot_of(step_u, step_v):
    if abs(step_u) > 1 or abs(step_v) > 1:
        return -1
    return (step_u + 1) * 3 + step_v + 1


def reference(x_blocks, pattern, alpha, beta):
    weights = pattern.astype(jnp.float32)[:, :, :, None, None]
    masked = x_blocks * weights
    block_shape = x_blocks.shape[:2] + x_blocks.shape[3:]
    sums = [jnp.zeros(block_shape, jnp.float32) for target in range(9)]
    for source, (step_u, step_v) in enumerate(STENCIL):
        shifted = jnp.roll(masked, (-step_u, -step_v), axis=(0, 1))
        left = masked[:, :, source]
        for target, (goal_u, goal_v) in enumerate(STENCIL):
            other = slot_of(goal_u - step_u, goal_v - step_v)
            if other >= 0:
                sums[target] = sums[target] + jnp.einsum("uvpm,uvmq->uvpq", left, shifted[:, :, other], precision=lax.Precision.HIGHEST)
    product = jnp.stack(sums, axis=2)
    updated = weights * (alpha * masked + beta * product)
    trace = jnp.sum(jnp.diagonal(updated[:, :, 4], axis1=2, axis2=3)) / (NU * NV)
    return updated, trace
```

```python
import functools

import jax
import jax.numpy as jnp
from jax import lax
from jax.experimental import pallas as pl
from jax.experimental.pallas import tpu as pltpu
from jax.sharding import PartitionSpec as P

CR, MID, TW = 0, 1, 2
AXES = ("row", "col")
B = 128
F32 = jnp.float32
BF16 = jnp.bfloat16
VMEM_LIMIT = 24 * 1024 * 1024
PARAMS = pltpu.CompilerParams(vmem_limit_bytes=VMEM_LIMIT)

CROSS1 = [(CR, 0, -1), (CR, 0, 0), (CR, 3, 0), (CR, 3, 1), (CR, 0, 1), (CR, 1, 1), (CR, 2, 1), (CR, "m", 0)]
CROSS2 = [(MID, 0, -1), (MID, 0, 0), (MID, 3, 0), (MID, 3, 1), (CR, 1, -1), (CR, 2, -1), (CR, 3, -1), (CR, "n", 0)]
CROSS3 = [(MID, 0, 1), (MID, 1, -1), (MID, 1, 0), (MID, 1, 1), (MID, 2, -1), (MID, 2, 0), (MID, 2, 1), (MID, 3, -1)]
TWIN = [(TW, v, j) for v in range(4) for j in (-1, 0, 1)] + [(MID, v, j) for v in range(4) for j in (-1, 0, 1)]
EAST1 = [(k, 3, 1) for k in (CR, MID, TW)]
EAST2 = [(k, 3, 0) for k in (CR, MID, TW)]
WEST = [(k, 0, j) for k in (CR, MID, TW) for j in (-1, 0)]


def parity():
    return lax.rem(lax.axis_index("row"), 2)


def slot(kind, dv, odd):
    base = {CR: 6 * odd, MID: 3, TW: 6 - 6 * odd}[kind]
    return base + dv + 1


def cell(v, odd):
    if isinstance(v, str):
        return 1 + odd if v == "m" else 2 - odd
    return v


def weight(pat, v, s):
    return pat[0, v, s].astype(F32)


def own(x, pat, kind, v, dv, odd):
    s = slot(kind, dv, odd)
    v = cell(v, odd)
    return x[0, v, s] * weight(pat, v, s)


def split(block):
    high = block.astype(BF16)
    return high, (block - high.astype(F32)).astype(BF16)


def dot3(left, right):
    def side(blocks, part):
        return jnp.concatenate([jnp.concatenate([b[part] for b in line], axis=1) for line in blocks], axis=0)

    lh, ll, rh, rl = side(left, 0), side(left, 1), side(right, 0), side(right, 1)
    return jnp.dot(
        jnp.concatenate([lh, lh, ll], axis=1), jnp.concatenate([rh, rl, rh], axis=0), preferred_element_type=F32
    )


def put(ref, index, block):
    ref[pl.ds(index * B, B), :] = block


def get(ref, index):
    return ref[pl.ds(index * B, B), :]


def put_present(ref, count, pat):
    row = lax.broadcasted_iota(jnp.int32, (8, B), 0)
    value = jnp.zeros((8, B), F32)
    for v in range(4):
        value = jnp.where(row == v, weight(pat, v, 4), value)
    ref[pl.ds(count * B, 8), :] = value


def get_present(ref, count, v):
    return ref[pl.ds(count * B + v, 1), :]


def pack_kernel(messages, present, x, pat, *outs):
    odd = parity()
    for out, message, extra in zip(outs, messages, present):
        for i, (kind, v, dv) in enumerate(message):
            put(out, i, own(x, pat, kind, v, dv, odd))
        if extra:
            put_present(out, len(message), pat)


def pack(x, pat, messages, present):
    shapes = [jax.ShapeDtypeStruct((len(m) * B + 8 * e, B), F32) for m, e in zip(messages, present)]
    return pl.pallas_call(
        functools.partial(pack_kernel, messages, present),
        out_shape=shapes,
        in_specs=[pl.BlockSpec(memory_space=pltpu.VMEM), pl.BlockSpec(memory_space=pltpu.SMEM)],
        out_specs=[pl.BlockSpec(memory_space=pltpu.VMEM)] * len(shapes),
        compiler_params=PARAMS,
        cost_estimate=pl.CostEstimate(flops=0, bytes_accessed=4000000, transcendentals=0),
    )(x, pat)


def trace_kernel(x, pat, alpha, beta, c1, tw, e1, out):
    odd = parity()
    mine = functools.partial(own, x, pat, odd=odd)
    present = lambda v: weight(pat, v, 4)
    pairs = []
    for v in range(4):
        pairs.append((1.0, mine(MID, v, 0), mine(MID, v, 0)))
    for v in range(3):
        pairs.append((present(v) + present(v + 1), mine(MID, v, 1), mine(MID, v + 1, -1)))
    west = get_present(e1, 3, 3)
    pairs.append((west + present(0), mine(MID, 0, -1), get(e1, 1)))
    middle = 2 - odd
    for kind, ref, blocks, count in ((CR, c1, CROSS1, 8), (TW, tw, TWIN, 24)):
        far = functools.partial(get_present, ref, count)
        take = lambda v, dv: get(ref, blocks.index((kind, v, dv)))
        pairs.append((present(0), mine(kind, 0, 0), take(0, 0)))
        pairs.append((present(3), mine(kind, 3, 0), take(3, 0)))
        for w in range(3):
            pairs.append((present(w + 1) + far(w), mine(kind, w + 1, -1), take(w, 1)))
        if kind == CR:
            center = get(c1, blocks.index((CR, "m", 0)))
        else:
            center = tw[pl.ds(pl.multiple_of((middle * 3 + 1) * B, B), B), :]
        far_middle = jnp.where(odd == 1, far(1), far(2))
        pairs.append((present(middle) + far_middle, mine(kind, middle, 0), center))
        pairs.append((west + far(0), get(e1, kind), take(0, -1)))
    total = jnp.zeros((B, B), F32)
    for start in range(0, len(pairs), 11):
        part = pairs[start : start + 11]
        total += dot3([[split(a * w) for w, a, _ in part]], [[split(b)] for _, _, b in part])
    linear = mine(MID, 0, 0) + mine(MID, 1, 0) + mine(MID, 2, 0) + mine(MID, 3, 0)
    value = alpha[0] * linear + beta[0] * total
    rows = lax.broadcasted_iota(jnp.int32, (B, B), 0)
    columns = lax.broadcasted_iota(jnp.int32, (B, B), 1)
    line = jnp.sum(jnp.where(rows == columns, value, 0.0), axis=0, keepdims=True)
    out[...] = jnp.broadcast_to(line, (B, B))


def near_kernel(x, pat, tw, acc, oh, ol, th, tl):
    odd = parity()
    for v in range(4):
        for kind in (CR, MID, TW):
            for j in (-1, 0, 1):
                i = kind * 12 + v * 3 + j + 1
                oh[i], ol[i] = split(own(x, pat, kind, v, j, odd))
    for i in range(24):
        th[i], tl[i] = split(get(tw, i))
    mine = lambda kind, v, j: (oh[kind * 12 + v * 3 + j + 1], ol[kind * 12 + v * 3 + j + 1])
    far = lambda kind, v, j: (th[(kind == MID) * 12 + v * 3 + j + 1], tl[(kind == MID) * 12 + v * 3 + j + 1])
    seen = set()

    def add(kind, v, sv, block):
        i = kind * 12 + v * 3 + sv + 1
        if i in seen:
            acc[i] += block
        else:
            seen.add(i)
            acc[i] = block

    for w in range(4):
        for t in (0, -1, 1):
            targets = [(w - a, a) for a in (-1, 0, 1) if 0 <= w - a < 4 and -1 <= a + t <= 1]
            left = [[mine(MID, v, a), mine(TW, v, a)] for v, a in targets]
            right = [[mine(MID, w, t), mine(TW, w, t)], [far(TW, w, t), far(MID, w, t)]]
            both = dot3(left, right)
            only = dot3([line[:1] for line in left], [[mine(CR, w, t)]])
            for n, (v, a) in enumerate(targets):
                rows = slice(n * B, (n + 1) * B)
                add(MID, v, a + t, both[rows, :B])
                add(TW, v, a + t, both[rows, B:])
                add(CR, v, a + t, only[rows])


def final_kernel(x, pat, alpha, beta, acc, c1, c2, c3, e1, e2, we, fe, fw, tc, out):
    odd = parity()
    mine = lambda kind, v, j: split(own(x, pat, kind, v, j, odd))
    part = lambda ref, i: split(get(ref, i))
    index = lambda kind, v, sv: kind * 12 + v * 3 + sv + 1

    def spread(left, rights, places):
        result = dot3([[left]], [rights])
        for n, (kind, v, sv) in enumerate(places):
            acc[index(kind, v, sv)] += result[:, n * B : (n + 1) * B]

    kinds = (CR, MID, TW)
    spread(mine(MID, 0, -1), [part(ref, k) for ref in (e2, e1) for k in kinds], [(k, 0, s) for s in (-1, 0) for k in kinds])
    spread(mine(MID, 3, 1), [part(we, i) for i in range(6)], [(k, 3, s) for k in kinds for s in (0, 1)])
    spread(mine(TW, 0, -1), [part(tc, i) for i in range(4)], [(MID, 0, -1), (MID, 0, 0), (TW, 0, -1), (TW, 0, 0)])
    spread(mine(TW, 3, 1), [part(tc, i) for i in range(4, 8)], [(MID, 3, 0), (MID, 3, 1), (TW, 3, 0), (TW, 3, 1)])
    spread(mine(CR, 0, -1), [part(fe, i) for i in range(4)], [(MID, 0, -1), (MID, 0, 0), (CR, 0, -1), (CR, 0, 0)])
    spread(mine(CR, 3, 1), [part(fw, i) for i in range(4)], [(MID, 3, 0), (MID, 3, 1), (CR, 3, 0), (CR, 3, 1)])

    def center(w):
        m, n = get(c1, 7), get(c2, 7)
        return split(jnp.where(odd == 1, m, n) if w == 1 else jnp.where(odd == 1, n, m))

    def far(kind, w, t):
        key = (kind, w, t)
        for ref, blocks in ((c1, CROSS1), (c2, CROSS2), (c3, CROSS3)):
            if key in blocks:
                return part(ref, blocks.index(key))
        return center(w)

    lefts = {(v, a): mine(CR, v, a) for v in range(4) for a in (-1, 0, 1)}
    for w in range(4):
        for t in (0, -1, 1):
            targets = [(w - a, a) for a in (-1, 0, 1) if 0 <= w - a < 4 and -1 <= a + t <= 1]
            result = dot3([[lefts[key]] for key in targets], [[far(CR, w, t), far(MID, w, t)]])
            for n, (v, a) in enumerate(targets):
                rows = slice(n * B, (n + 1) * B)
                acc[index(MID, v, a + t)] += result[rows, :B]
                acc[index(CR, v, a + t)] += result[rows, B:]
    for v in range(4):
        for kind in kinds:
            for sv in (-1, 0, 1):
                s = slot(kind, sv, odd)
                p = weight(pat, v, s)
                out[0, v, s] = p * (alpha[0] * (p * x[0, v, s]) + beta[0] * acc[index(kind, v, sv)])


def body(x, pat, alpha, beta):
    rows, columns = lax.axis_size("row"), lax.axis_size("col")

    def moved(message, step):
        pairs = []
        for r in range(rows):
            for c in range(columns):
                r2, c2 = step(r, c)
                pairs.append((r * columns + c, (r2 % rows) * columns + c2 % columns))
        return lax.ppermute(message, AXES, pairs)

    cross = lambda r, c: (r - 1 if r % 2 == 0 else r + 1, c)
    twin = lambda r, c: (r ^ 1, c)
    east = lambda r, c: (r, c + 1)
    west = lambda r, c: (r, c - 1)
    alpha, beta = alpha.reshape(1), beta.reshape(1)
    vmem = pl.BlockSpec(memory_space=pltpu.VMEM)
    smem = pl.BlockSpec(memory_space=pltpu.SMEM)

    first = pack(x, pat, [CROSS1, EAST1], [1, 1])
    c1 = moved(first[0], cross)
    e1 = moved(first[1], east)
    second = pack(x, pat, [TWIN, CROSS2, WEST, EAST2, CROSS3], [1, 0, 0, 0, 0])
    tw = moved(second[0], twin)
    c2 = moved(second[1], cross)
    we = moved(second[2], west)
    e2 = moved(second[3], east)
    c3 = moved(second[4], cross)

    shares = pl.pallas_call(
        trace_kernel,
        out_shape=jax.ShapeDtypeStruct((B, B), F32),
        in_specs=[vmem, smem, smem, smem, vmem, vmem, vmem],
        out_specs=vmem,
        compiler_params=PARAMS,
        cost_estimate=pl.CostEstimate(flops=300000000, bytes_accessed=4000000, transcendentals=0),
    )(x, pat, alpha, beta, c1, tw, e1)
    total = jnp.sum(lax.all_to_all(shares, AXES, 0, 0))
    trace = total / (rows * columns * x.shape[1])

    fe = moved(jnp.concatenate([c1[2 * B : 4 * B], c2[2 * B : 4 * B]]), east)
    fw = moved(jnp.concatenate([c1[: 2 * B], c2[: 2 * B]]), west)
    corner = [e2[2 * B : 3 * B], e1[2 * B : 3 * B], e2[B : 2 * B], e1[B : 2 * B], we[4 * B : 6 * B], we[2 * B : 4 * B]]
    tc = moved(jnp.concatenate(corner), twin)

    acc = pl.pallas_call(
        near_kernel,
        out_shape=jax.ShapeDtypeStruct((36, B, B), F32),
        in_specs=[vmem, smem, vmem],
        out_specs=vmem,
        scratch_shapes=[pltpu.VMEM((36, B, B), BF16)] * 2 + [pltpu.VMEM((24, B, B), BF16)] * 2,
        compiler_params=PARAMS,
        cost_estimate=pl.CostEstimate(flops=1500000000, bytes_accessed=8000000, transcendentals=0),
    )(x, pat, tw)

    updated = pl.pallas_call(
        final_entry,
        out_shape=jax.ShapeDtypeStruct(x.shape, F32),
        in_specs=[vmem, smem, smem, smem] + [vmem] * 10,
        out_specs=vmem,
        scratch_shapes=[pltpu.VMEM((36, B, B), F32)],
        compiler_params=PARAMS,
        cost_estimate=pl.CostEstimate(flops=1000000000, bytes_accessed=12000000, transcendentals=0),
    )(x, pat, alpha, beta, acc, c1, c2, c3, e1, e2, we, fe, fw, tc)
    return (updated, trace)


def final_entry(x, pat, alpha, beta, start, *rest):
    *messages, out, acc = rest
    acc[...] = start[...]
    final_kernel(x, pat, alpha, beta, acc, *messages, out)


def solution(mesh):
    placed = (P("row", "col", None, None, None), P("row", "col", None), P(), P())
    return jax.shard_map(
        body,
        mesh=mesh,
        in_specs=placed,
        out_specs=(P("row", "col", None, None, None), P()),
        check_vma=False,
    )
```

```python
import functools

import jax
import jax.numpy as jnp
from jax import lax
from jax.experimental import pallas as pl
from jax.experimental.pallas import tpu as pltpu
from jax.sharding import PartitionSpec as P

CR, TW, MID = KINDS = (0, 1, 2)
AXES = ("row", "col")
B = 128
F32 = jnp.float32
BF16 = jnp.bfloat16
ANY = pl.BlockSpec(memory_space=pl.ANY)
VMEM = pl.BlockSpec(memory_space=pltpu.VMEM)
FAR = None
SMEM = pl.BlockSpec(memory_space=pltpu.SMEM)


def at(kind, v, j):
    return kind * 12 + v * 3 + j + 1


FIRST = [0, 1, 2, 4, 5, 7, 8, 10, 11]
SECOND = [3, 6, 9]
HEAD = 8


def slot(kind, dv, odd):
    base = {CR: 6 * odd, MID: 3, TW: 6 - 6 * odd}[kind]
    return base + dv + 1


def weight(pat, v, s):
    return pat[0, v, s].astype(F32)


def split(block):
    high = block.astype(BF16)
    return high, (block - high.astype(F32)).astype(BF16)


def dot3(left, right):
    def side(blocks, part):
        return jnp.concatenate([jnp.concatenate([b[part] for b in line], axis=1) for line in blocks], axis=0)

    lh, ll, rh, rl = side(left, 0), side(left, 1), side(right, 0), side(right, 1)
    return jnp.dot(
        jnp.concatenate([lh, lh, ll], axis=1), jnp.concatenate([rh, rl, rh], axis=0), preferred_element_type=F32
    )


def get(ref, i, head=0):
    return ref[pl.ds(head + i * B, B), :]


def put(ref, i, block, head=0):
    ref[pl.ds(head + i * B, B), :] = block


class Copies:
    def __init__(self, sems):
        self.sems, self.count = sems, 0

    def start(self, source, target):
        copy = pltpu.make_async_copy(source, target, self.sems.at[self.count])
        self.count += 1
        copy.start()
        return copy


def pack_kernel(x, pat, c1, ea, tw, c2, we, rest, stage, table, sems):
    odd = lax.rem(lax.axis_index("row"), 2)
    dma = Copies(sems)
    order = (0, 3, 1, 2)
    table_load = dma.start(pat, table)
    loads = {v: dma.start(x.at[0, v], stage.at[v]) for v in order}
    table_load.wait()
    rows = lax.broadcasted_iota(jnp.int32, (HEAD, B), 0)
    present = jnp.zeros((HEAD, B), F32)
    for v in range(4):
        present = jnp.where(rows == v, weight(table, v, 4), present)
    for ref in (c1, ea, tw):
        ref[pl.ds(0, HEAD), :] = present

    for v in order:
        loads[v].wait()
        for kind in KINDS:
            for j in (-1, 0, 1):
                s = slot(kind, j, odd)
                block = stage[v, s] * weight(table, v, s)
                i = at(kind, v, j)
                if kind != CR:
                    put(tw, i - 12, block, HEAD)
                elif i in FIRST:
                    put(c1, FIRST.index(i), block, HEAD)
                else:
                    put(c2, SECOND.index(i), block)
                    put(rest, SECOND.index(i), block)
                if kind == MID:
                    put(c2, 3 + i - 24, block)
                if v == 3 and j >= 0:
                    put(ea, 2 * kind + j, block, HEAD)
                if v == 0 and j < 1:
                    put(we, 2 * kind + j + 1, block)


def near_kernel(alpha, beta, c1m, rest, twm, tw, acc, lefts, pairs, few, lh, ll, sh, sl, rh, rl):
    def own(kind, v, j):
        i = at(kind, v, j)
        if kind != CR:
            return get(twm, i - 12, HEAD)
        return get(c1m, FIRST.index(i), HEAD) if i in FIRST else get(rest, SECOND.index(i))

    sources = {at(CR, v, a): at(CR, v, a) for v in range(4) for a in (-1, 0, 1)}
    sources.update({at(TW, 0, -1): 12, at(TW, 3, 1): 13, at(MID, 0, -1): 14, at(MID, 3, 1): 15})

    def prepare(v):
        for kind in KINDS:
            for j in (-1, 0, 1):
                i = at(kind, v, j)
                block = own(kind, v, j)
                acc[v * 9 + kind * 3 + j + 1] = alpha[...] * block
                rh[i], rl[i] = split(block)
                high, low = split(beta[...] * block)
                if kind != CR:
                    lh[i - 12], ll[i - 12] = high, low
                if i in sources:
                    lefts[sources[i]], lefts[16 + sources[i]] = high, low
        for j in (-1, 0, 1):
            for kind in (TW, MID):
                i = at(kind, v, j) - 12
                sh[i], sl[i] = split(get(tw, i, HEAD))

    left = lambda kind, v, j: (lh[at(kind, v, j) - 12], ll[at(kind, v, j) - 12])
    mine = lambda kind, v, j: (rh[at(kind, v, j)], rl[at(kind, v, j)])
    theirs = lambda kind, v, j: (sh[at(kind, v, j) - 12], sl[at(kind, v, j) - 12])

    def add(kind, v, sv, block):
        acc[v * 9 + kind * 3 + sv + 1] += block

    for w in range(4):
        prepare(w)
    for w in range(4):
        for t in (0, -1, 1):
            targets = [(w - a, a) for a in (-1, 0, 1) if 0 <= w - a < 4 and -1 <= a + t <= 1]
            lines = [[left(MID, v, a), left(TW, v, a)] for v, a in targets]
            right = [[mine(MID, w, t), mine(TW, w, t)], [theirs(TW, w, t), theirs(MID, w, t)]]
            both = dot3(lines, right)
            only = dot3([line[:1] for line in lines], [[mine(CR, w, t)]])
            for n, (v, a) in enumerate(targets):
                rows = slice(n * B, (n + 1) * B)
                add(MID, v, a + t, both[rows, :B])
                add(TW, v, a + t, both[rows, B:])
                add(CR, v, a + t, only[rows])
    present = lambda v: twm[pl.ds(v, 1), :]
    other = lambda v: tw[pl.ds(v, 1), :]
    listed = []
    for v in range(4):
        listed.append((own(MID, v, 0), mine(MID, v, 0)))
        listed.append((own(TW, v, 0) * present(v), theirs(TW, v, 0)))
    for v in range(3):
        listed.append((own(MID, v, 1) * (present(v) + present(v + 1)), mine(MID, v + 1, -1)))
        listed.append((own(TW, v + 1, -1) * (present(v + 1) + other(v)), theirs(TW, v, 1)))
    value = beta[...] * dot3([[split(a) for a, _ in listed]], [[b] for _, b in listed])
    for v in range(4):
        value += alpha[...] * own(MID, v, 0)
    pairs[...] = value
    few[pl.ds(0, HEAD), :] = twm[pl.ds(0, HEAD), :]
    few[pl.ds(HEAD, HEAD), :] = tw[pl.ds(0, HEAD), :]
    kept = [own(CR, v, 0) for v in range(4)] + [own(CR, v, -1) for v in (1, 2, 3)] + [own(MID, 0, -1), get(tw, 0, HEAD)]
    for i, block in enumerate(kept):
        put(few, i, block, 2 * HEAD)


def trace_kernel(beta, pairs, few, c1, ea, out):
    own = lambda v: few[pl.ds(v, 1), :]
    far = lambda v: c1[pl.ds(v, 1), :]
    west = ea[pl.ds(3, 1), :]
    kept = lambda i: get(few, i, 2 * HEAD)
    listed = []
    for v in range(4):
        listed.append((own(v), kept(v), get(c1, 2 * v + 1, HEAD)))
    for v in range(3):
        listed.append((own(v + 1) + far(v), kept(4 + v), get(c1, 2 * v + 2, HEAD)))
    listed.append((west + own(0), get(ea, 2 * MID + 1, HEAD), kept(7)))
    listed.append((west + far(0), get(ea, 2 * CR + 1, HEAD), get(c1, 0, HEAD)))
    listed.append((west + few[pl.ds(HEAD, 1), :], get(ea, 2 * TW + 1, HEAD), kept(8)))
    value = pairs[...] + beta[...] * dot3([[split(a * w) for w, a, _ in listed]], [[split(b)] for _, _, b in listed])
    rows = lax.broadcasted_iota(jnp.int32, (B, B), 0)
    columns = lax.broadcasted_iota(jnp.int32, (B, B), 1)
    line = jnp.sum(jnp.where(rows == columns, value, 0.0), axis=0, keepdims=True)
    out[...] = jnp.broadcast_to(line, (B, B))


def sum_kernel(scale, shares, after, out):
    out[0, 0] = jnp.sum(shares[...]) * scale


def corner_kernel(ea, we, after, cc, tc):
    for out, toward in ((cc, CR), (tc, TW)):
        for i, k in enumerate((toward, MID)):
            for n in (0, 1):
                put(out, 2 * i + n, get(ea, 2 * k + n, HEAD))
                put(out, 4 + 2 * i + n, get(we, 2 * k + n))


def final_kernel(pat, lefts, acc, c1, c2, ea, we, cc, tc, out, total, stage, sems):
    odd = lax.rem(lax.axis_index("row"), 2)
    dma = Copies(sems)
    left = lambda i: (lefts[i], lefts[16 + i])
    seen = set()

    def add(kind, v, sv, block):
        i = v * 9 + kind * 3 + sv + 1
        total[i] = (total[i] if i in seen else acc[i]) + block
        seen.add(i)

    def spread(source, rights, places):
        result = dot3([[left(source)]], [[split(block) for block in rights]])
        for n, (kind, v, sv) in enumerate(places):
            add(kind, v, sv, result[:, n * B : (n + 1) * B])

    spread(14, [get(ea, i, HEAD) for i in range(6)], [(k, 0, s) for k in KINDS for s in (-1, 0)])
    spread(15, [get(we, i) for i in range(6)], [(k, 3, s) for k in KINDS for s in (0, 1)])
    spread(12, [get(tc, i) for i in range(4)], [(MID, 0, -1), (MID, 0, 0), (TW, 0, -1), (TW, 0, 0)])
    spread(13, [get(tc, 4 + i) for i in range(4)], [(MID, 3, 0), (MID, 3, 1), (TW, 3, 0), (TW, 3, 1)])
    spread(at(CR, 0, -1), [get(cc, i) for i in range(4)], [(MID, 0, -1), (MID, 0, 0), (CR, 0, -1), (CR, 0, 0)])
    spread(at(CR, 3, 1), [get(cc, 4 + i) for i in range(4)], [(MID, 3, 0), (MID, 3, 1), (CR, 3, 0), (CR, 3, 1)])

    def far(w, t):
        i = at(CR, w, t)
        return get(c1, FIRST.index(i), HEAD) if i in FIRST else get(c2, SECOND.index(i))

    stores = []

    def finish(v):
        for kind in KINDS:
            for sv in (-1, 0, 1):
                i, s = v * 9 + kind * 3 + sv + 1, slot(kind, sv, odd)
                stage[v, s] = weight(pat, v, s) * (total[i] if i in seen else acc[i])
        stores.append(dma.start(stage.at[v], out.at[0, v]))

    for w in range(4):
        for t in (0, -1, 1):
            targets = [(w - a, a) for a in (-1, 0, 1) if 0 <= w - a < 4 and -1 <= a + t <= 1]
            lines = [[left(at(CR, v, a))] for v, a in targets]
            result = dot3(lines, [[split(far(w, t)), split(get(c2, 3 + w * 3 + t + 1))]])
            for n, (v, a) in enumerate(targets):
                rows = slice(n * B, (n + 1) * B)
                add(MID, v, a + t, result[rows, :B])
                add(CR, v, a + t, result[rows, B:])
        if w >= 1:
            finish(w - 1)
    finish(3)
    for copy in stores:
        copy.wait()


def body(x, pat, alpha, beta):
    rows, columns = lax.axis_size("row"), lax.axis_size("col")

    def moved(message, step):
        pairs = []
        for r in range(rows):
            for c in range(columns):
                r2, c2 = step(r, c)
                pairs.append((r * columns + c, (r2 % rows) * columns + c2 % columns))
        return lax.ppermute(message, AXES, pairs)

    def call(kernel, outs, args, specs, size, scratch=()):
        spaces = [pltpu.HBM if s is ANY or a is pat else None for a, s in zip(args, specs)]
        return pl.pallas_call(
            kernel,
            out_shape=[pltpu.HBM(o.shape, o.dtype) if s is ANY or s is FAR else o for o, s in outs],
            in_specs=specs,
            out_specs=[VMEM if s is FAR else s for _, s in outs],
            scratch_shapes=scratch,
            compiler_params=pltpu.CompilerParams(vmem_limit_bytes=size * 1024 * 1024),
            cost_estimate=pl.CostEstimate(flops=1000, bytes_accessed=1000, transcendentals=0),
        )(*[pltpu.with_memory_space_constraint(a, m) if m else a for a, m in zip(args, spaces)])

    shape = lambda *dims, dtype=F32: jax.ShapeDtypeStruct(dims, dtype)
    lines = lambda count, head=0: shape(count * B + head, B)
    sems = lambda count: pltpu.SemaphoreType.DMA((count,))
    far = lambda a: pltpu.with_memory_space_constraint(a, pltpu.HBM)
    vmem = lambda *dims, dtype=F32: pltpu.VMEM(dims, dtype)
    crossing = lambda r: r - 1 if r % 2 == 0 else r + 1
    cross = lambda r, c: (crossing(r), c)
    twin = lambda r, c: (r ^ 1, c)
    east = lambda r, c: (r, c + 1)
    west = lambda r, c: (r, c - 1)
    alpha, beta = alpha.reshape(1, 1), beta.reshape(1, 1)

    *messages, rest = call(
        pack_kernel,
        [(lines(9, HEAD), VMEM), (lines(6, HEAD), VMEM), (lines(24, HEAD), VMEM), (lines(15), VMEM), (lines(6), VMEM), (lines(3), VMEM)],
        (x, pat),
        [ANY, ANY],
        10,
        [vmem(4, 9, B, B), pltpu.SMEM(pat.shape, jnp.int32), sems(5)],
    )
    c1, ea, tw, c2, we = [moved(m, s) for m, s in zip(messages, [cross, east, twin, cross, west])]
    c1m, _, twm = messages[:3]
    acc, lefts, pairs, few = call(
        near_kernel,
        [(shape(36, B, B), FAR), (shape(32, B, B, dtype=BF16), FAR), (shape(B, B), VMEM), (lines(9, 2 * HEAD), VMEM)],
        (alpha, beta, c1m, rest, twm, tw),
        [VMEM] * 6,
        14,
        [vmem(n, B, B, dtype=BF16) for n in (24, 24, 24, 24, 36, 36)],
    )
    (shares,) = call(
        trace_kernel,
        [(shape(B, B), VMEM)],
        (beta, pairs, few, c1, ea),
        [VMEM] * 5,
        4,
    )
    gathered = lax.all_to_all(shares, AXES, 0, 0)
    corners = call(corner_kernel, [(lines(8), VMEM)] * 2, (ea, we, pairs), [VMEM] * 3, 4)
    cc, tc = moved(corners[0], cross), moved(corners[1], twin)
    (updated,) = call(
        final_kernel,
        [(shape(*x.shape), ANY)],
        (pat, far(lefts), far(acc), c1, c2, ea, we, cc, tc),
        [SMEM] + [VMEM] * 8,
        14,
        [vmem(36, B, B), vmem(4, 9, B, B), sems(4)],
    )
    scale = 1.0 / (rows * columns * x.shape[1])
    (trace,) = call(functools.partial(sum_kernel, scale), [(shape(1, 1), SMEM)], (gathered, updated), [VMEM, ANY], 2)
    return (updated, trace.reshape(()))


def solution(mesh):
    placed = (P("row", "col", None, None, None), P("row", "col", None), P(), P())
    return jax.shard_map(
        body,
        mesh=mesh,
        in_specs=placed,
        out_specs=(P("row", "col", None, None, None), P()),
        check_vma=False,
    )
```

```python
import functools

import jax
import jax.numpy as jnp
from jax import lax
from jax.experimental import pallas as pl
from jax.experimental.pallas import tpu as pltpu
from jax.sharding import PartitionSpec as P

CR, TW, MID = KINDS = (0, 1, 2)
AXES = ("row", "col")
B = 128
F32 = jnp.float32
BF16 = jnp.bfloat16
ANY = pl.BlockSpec(memory_space=pl.ANY)
VMEM = pl.BlockSpec(memory_space=pltpu.VMEM)
FAR = None
SMEM = pl.BlockSpec(memory_space=pltpu.SMEM)


def at(kind, v, j):
    return kind * 12 + v * 3 + j + 1


HEAD = 8


def slot(kind, dv, odd):
    base = {CR: 6 * odd, MID: 3, TW: 6 - 6 * odd}[kind]
    return base + dv + 1


def weight(pat, v, s):
    return pat[0, v, s].astype(F32)


def split(block):
    high = block.astype(BF16)
    return high, (block - high.astype(F32)).astype(BF16)


def dot3(left, right):
    def side(blocks, part):
        return jnp.concatenate([jnp.concatenate([b[part] for b in line], axis=1) for line in blocks], axis=0)

    lh, ll, rh, rl = side(left, 0), side(left, 1), side(right, 0), side(right, 1)
    return jnp.dot(
        jnp.concatenate([lh, lh, ll], axis=1), jnp.concatenate([rh, rl, rh], axis=0), preferred_element_type=F32
    )


def get(ref, i, head=0):
    return ref[pl.ds(head + i * B, B), :]


def put(ref, i, block, head=0):
    ref[pl.ds(head + i * B, B), :] = block


class Copies:
    def __init__(self, sems):
        self.sems, self.count = sems, 0

    def start(self, source, target):
        copy = pltpu.make_async_copy(source, target, self.sems.at[self.count])
        self.count += 1
        copy.start()
        return copy


def pack_kernel(x, pat, c1, ea, tw, c2, we, stage, table, sems):
    odd = lax.rem(lax.axis_index("row"), 2)
    dma = Copies(sems)
    order = (0, 3, 1, 2)
    table_load = dma.start(pat, table)
    loads = {v: dma.start(x.at[0, v], stage.at[v]) for v in order}
    table_load.wait()
    rows = lax.broadcasted_iota(jnp.int32, (HEAD, B), 0)
    present = jnp.zeros((HEAD, B), F32)
    for v in range(4):
        present = jnp.where(rows == v, weight(table, v, 4), present)
    for ref in (c1, ea, tw):
        ref[pl.ds(0, HEAD), :] = present

    for v in order:
        loads[v].wait()
        for kind in KINDS:
            for j in (-1, 0, 1):
                s = slot(kind, j, odd)
                block = stage[v, s] * weight(table, v, s)
                i = at(kind, v, j)
                if kind == CR:
                    put(c1, i, block, HEAD)
                else:
                    put(tw, i - 12, block, HEAD)
                if kind == MID:
                    put(c2, i - 24, block)
                if v == 3 and j >= 0:
                    put(ea, 2 * kind + j, block, HEAD)
                if v == 0 and j < 1:
                    put(we, 2 * kind + j + 1, block)


def near_kernel(alpha, beta, c1m, twm, tw, acc, lefts, pairs, few, lh, ll, sh, sl, rh, rl):
    def own(kind, v, j):
        i = at(kind, v, j)
        return get(c1m, i, HEAD) if kind == CR else get(twm, i - 12, HEAD)

    sources = {at(CR, v, a): at(CR, v, a) for v in range(4) for a in (-1, 0, 1)}
    sources.update({at(TW, 0, -1): 12, at(TW, 3, 1): 13, at(MID, 0, -1): 14, at(MID, 3, 1): 15})

    def prepare(v):
        for kind in KINDS:
            for j in (-1, 0, 1):
                i = at(kind, v, j)
                block = own(kind, v, j)
                acc[v * 9 + kind * 3 + j + 1] = alpha[...] * block
                rh[i], rl[i] = split(block)
                high, low = split(beta[...] * block)
                if kind != CR:
                    lh[i - 12], ll[i - 12] = high, low
                if i in sources:
                    lefts[sources[i]], lefts[16 + sources[i]] = high, low
        for j in (-1, 0, 1):
            for kind in (TW, MID):
                i = at(kind, v, j) - 12
                sh[i], sl[i] = split(get(tw, i, HEAD))

    left = lambda kind, v, j: (lh[at(kind, v, j) - 12], ll[at(kind, v, j) - 12])
    mine = lambda kind, v, j: (rh[at(kind, v, j)], rl[at(kind, v, j)])
    theirs = lambda kind, v, j: (sh[at(kind, v, j) - 12], sl[at(kind, v, j) - 12])

    def add(kind, v, sv, block):
        acc[v * 9 + kind * 3 + sv + 1] += block

    for w in range(4):
        prepare(w)
    for w in range(4):
        for t in (0, -1, 1):
            targets = [(w - a, a) for a in (-1, 0, 1) if 0 <= w - a < 4 and -1 <= a + t <= 1]
            lines = [[left(MID, v, a), left(TW, v, a)] for v, a in targets]
            right = [[mine(MID, w, t), mine(TW, w, t)], [theirs(TW, w, t), theirs(MID, w, t)]]
            both = dot3(lines, right)
            only = dot3([line[:1] for line in lines], [[mine(CR, w, t)]])
            for n, (v, a) in enumerate(targets):
                rows = slice(n * B, (n + 1) * B)
                add(MID, v, a + t, both[rows, :B])
                add(TW, v, a + t, both[rows, B:])
                add(CR, v, a + t, only[rows])
    present = lambda v: twm[pl.ds(v, 1), :]
    other = lambda v: tw[pl.ds(v, 1), :]
    listed = []
    for v in range(4):
        listed.append((own(MID, v, 0), mine(MID, v, 0)))
        listed.append((own(TW, v, 0) * present(v), theirs(TW, v, 0)))
    for v in range(3):
        listed.append((own(MID, v, 1) * (present(v) + present(v + 1)), mine(MID, v + 1, -1)))
        listed.append((own(TW, v + 1, -1) * (present(v + 1) + other(v)), theirs(TW, v, 1)))
    value = beta[...] * dot3([[split(a) for a, _ in listed]], [[b] for _, b in listed])
    for v in range(4):
        value += alpha[...] * own(MID, v, 0)
    pairs[...] = value
    few[pl.ds(0, HEAD), :] = twm[pl.ds(0, HEAD), :]
    few[pl.ds(HEAD, HEAD), :] = tw[pl.ds(0, HEAD), :]
    kept = [own(CR, v, 0) for v in range(4)] + [own(CR, v, -1) for v in (1, 2, 3)] + [own(MID, 0, -1), get(tw, 0, HEAD)]
    for i, block in enumerate(kept):
        put(few, i, block, 2 * HEAD)


def middle_kernel(beta, pairs, few, c1, ea, we, cc, tc, shares):
    for out, toward in ((cc, CR), (tc, TW)):
        for i, k in enumerate((toward, MID)):
            for n in (0, 1):
                put(out, 2 * i + n, get(ea, 2 * k + n, HEAD))
                put(out, 4 + 2 * i + n, get(we, 2 * k + n))

    own = lambda v: few[pl.ds(v, 1), :]
    far = lambda v: c1[pl.ds(v, 1), :]
    west = ea[pl.ds(3, 1), :]
    kept = lambda i: get(few, i, 2 * HEAD)
    listed = []
    for v in range(4):
        listed.append((own(v), kept(v), get(c1, at(CR, v, 0), HEAD)))
    for v in range(3):
        listed.append((own(v + 1) + far(v), kept(4 + v), get(c1, at(CR, v, 1), HEAD)))
    listed.append((west + own(0), get(ea, 2 * MID + 1, HEAD), kept(7)))
    listed.append((west + far(0), get(ea, 2 * CR + 1, HEAD), get(c1, 0, HEAD)))
    listed.append((west + few[pl.ds(HEAD, 1), :], get(ea, 2 * TW + 1, HEAD), kept(8)))
    value = pairs[...] + beta[...] * dot3([[split(a * w) for w, a, _ in listed]], [[split(b)] for _, _, b in listed])
    rows = lax.broadcasted_iota(jnp.int32, (B, B), 0)
    columns = lax.broadcasted_iota(jnp.int32, (B, B), 1)
    line = jnp.sum(jnp.where(rows == columns, value, 0.0), axis=0, keepdims=True)
    shares[...] = jnp.broadcast_to(line, (B, B))


def sum_kernel(scale, shares, after, out):
    out[0, 0] = jnp.sum(shares[...]) * scale


def final_kernel(pat, lefts, acc, c1, c2, ea, we, cc, tc, out, total, stage, sems):
    odd = lax.rem(lax.axis_index("row"), 2)
    dma = Copies(sems)
    left = lambda i: (lefts[i], lefts[16 + i])
    seen = set()

    def add(kind, v, sv, block):
        i = v * 9 + kind * 3 + sv + 1
        total[i] = (total[i] if i in seen else acc[i]) + block
        seen.add(i)

    def spread(source, rights, places):
        result = dot3([[left(source)]], [[split(block) for block in rights]])
        for n, (kind, v, sv) in enumerate(places):
            add(kind, v, sv, result[:, n * B : (n + 1) * B])

    spread(14, [get(ea, i, HEAD) for i in range(6)], [(k, 0, s) for k in KINDS for s in (-1, 0)])
    spread(15, [get(we, i) for i in range(6)], [(k, 3, s) for k in KINDS for s in (0, 1)])
    spread(12, [get(tc, i) for i in range(4)], [(MID, 0, -1), (MID, 0, 0), (TW, 0, -1), (TW, 0, 0)])
    spread(13, [get(tc, 4 + i) for i in range(4)], [(MID, 3, 0), (MID, 3, 1), (TW, 3, 0), (TW, 3, 1)])
    spread(at(CR, 0, -1), [get(cc, i) for i in range(4)], [(MID, 0, -1), (MID, 0, 0), (CR, 0, -1), (CR, 0, 0)])
    spread(at(CR, 3, 1), [get(cc, 4 + i) for i in range(4)], [(MID, 3, 0), (MID, 3, 1), (CR, 3, 0), (CR, 3, 1)])

    stores = []

    def finish(v):
        for kind in KINDS:
            for sv in (-1, 0, 1):
                i, s = v * 9 + kind * 3 + sv + 1, slot(kind, sv, odd)
                stage[v, s] = weight(pat, v, s) * (total[i] if i in seen else acc[i])
        stores.append(dma.start(stage.at[v], out.at[0, v]))

    for w in range(4):
        for t in (0, -1, 1):
            targets = [(w - a, a) for a in (-1, 0, 1) if 0 <= w - a < 4 and -1 <= a + t <= 1]
            lines = [[left(at(CR, v, a))] for v, a in targets]
            result = dot3(lines, [[split(get(c1, at(CR, w, t), HEAD)), split(get(c2, at(CR, w, t)))]])
            for n, (v, a) in enumerate(targets):
                rows = slice(n * B, (n + 1) * B)
                add(MID, v, a + t, result[rows, :B])
                add(CR, v, a + t, result[rows, B:])
        if w >= 1:
            finish(w - 1)
    finish(3)
    for copy in stores:
        copy.wait()


def body(x, pat, alpha, beta):
    rows, columns = lax.axis_size("row"), lax.axis_size("col")

    def moved(message, step):
        pairs = []
        for r in range(rows):
            for c in range(columns):
                r2, c2 = step(r, c)
                pairs.append((r * columns + c, (r2 % rows) * columns + c2 % columns))
        return lax.ppermute(message, AXES, pairs)

    def call(kernel, outs, args, specs, size, scratch=()):
        spaces = [pltpu.HBM if s is ANY or a is pat else None for a, s in zip(args, specs)]
        return pl.pallas_call(
            kernel,
            out_shape=[pltpu.HBM(o.shape, o.dtype) if s is ANY or s is FAR else o for o, s in outs],
            in_specs=specs,
            out_specs=[VMEM if s is FAR else s for _, s in outs],
            scratch_shapes=scratch,
            compiler_params=pltpu.CompilerParams(vmem_limit_bytes=size * 1024 * 1024),
            cost_estimate=pl.CostEstimate(flops=1000, bytes_accessed=1000, transcendentals=0),
        )(*[pltpu.with_memory_space_constraint(a, m) if m else a for a, m in zip(args, spaces)])

    shape = lambda *dims, dtype=F32: jax.ShapeDtypeStruct(dims, dtype)
    lines = lambda count, head=0: shape(count * B + head, B)
    sems = lambda count: pltpu.SemaphoreType.DMA((count,))
    far = lambda a: pltpu.with_memory_space_constraint(a, pltpu.HBM)
    vmem = lambda *dims, dtype=F32: pltpu.VMEM(dims, dtype)
    crossing = lambda r: r - 1 if r % 2 == 0 else r + 1
    cross = lambda r, c: (crossing(r), c)
    twin = lambda r, c: (r ^ 1, c)
    east = lambda r, c: (r, c + 1)
    west = lambda r, c: (r, c - 1)
    alpha, beta = alpha.reshape(1, 1), beta.reshape(1, 1)

    messages = call(
        pack_kernel,
        [(lines(12, HEAD), VMEM), (lines(6, HEAD), VMEM), (lines(24, HEAD), VMEM), (lines(12), VMEM), (lines(6), VMEM)],
        (x, pat),
        [ANY, ANY],
        10,
        [vmem(4, 9, B, B), pltpu.SMEM(pat.shape, jnp.int32), sems(5)],
    )
    c1, ea, tw, c2, we = [moved(m, s) for m, s in zip(messages, [cross, east, twin, cross, west])]
    c1m, _, twm = messages[:3]
    acc, lefts, pairs, few = call(
        near_kernel,
        [(shape(36, B, B), FAR), (shape(32, B, B, dtype=BF16), FAR), (shape(B, B), VMEM), (lines(9, 2 * HEAD), VMEM)],
        (alpha, beta, c1m, twm, tw),
        [VMEM] * 5,
        14,
        [vmem(n, B, B, dtype=BF16) for n in (24, 24, 24, 24, 36, 36)],
    )
    *corners, shares = call(
        middle_kernel,
        [(lines(8), VMEM), (lines(8), VMEM), (shape(B, B), VMEM)],
        (beta, pairs, few, c1, ea, we),
        [VMEM] * 6,
        4,
    )
    cc, tc = moved(corners[0], cross), moved(corners[1], twin)
    gathered = lax.all_to_all(shares, AXES, 0, 0)
    (updated,) = call(
        final_kernel,
        [(shape(*x.shape), ANY)],
        (pat, far(lefts), far(acc), c1, c2, ea, we, cc, tc),
        [SMEM] + [VMEM] * 8,
        14,
        [vmem(36, B, B), vmem(4, 9, B, B), sems(4)],
    )
    scale = 1.0 / (rows * columns * x.shape[1])
    (trace,) = call(functools.partial(sum_kernel, scale), [(shape(1, 1), SMEM)], (gathered, updated), [VMEM, ANY], 2)
    return (updated, trace.reshape(()))


def solution(mesh):
    placed = (P("row", "col", None, None, None), P("row", "col", None), P(), P())
    return jax.shard_map(
        body,
        mesh=mesh,
        in_specs=placed,
        out_specs=(P("row", "col", None, None, None), P()),
        check_vma=False,
    )
```

```python
import functools

import jax
import jax.numpy as jnp
from jax import lax
from jax.experimental import pallas as pl
from jax.experimental.pallas import tpu as pltpu
from jax.sharding import PartitionSpec as P

CR, TW, MID = KINDS = (0, 1, 2)
AXES = ("row", "col")
B = 128
F32 = jnp.float32
BF16 = jnp.bfloat16
ANY = pl.BlockSpec(memory_space=pl.ANY)
VMEM = pl.BlockSpec(memory_space=pltpu.VMEM)
FAR = None
SMEM = pl.BlockSpec(memory_space=pltpu.SMEM)


def at(kind, v, j):
    return kind * 12 + v * 3 + j + 1


SIDE = {CR: 0, MID: 2, TW: 4}
HEAD = 8


def slot(kind, dv, odd):
    base = {CR: 6 * odd, MID: 3, TW: 6 - 6 * odd}[kind]
    return base + dv + 1


def weight(pat, v, s):
    return pat[0, v, s].astype(F32)


def split(block):
    high = block.astype(BF16)
    return high, (block - high.astype(F32)).astype(BF16)


def dot3(left, right):
    def side(blocks, part):
        return jnp.concatenate([jnp.concatenate([b[part] for b in line], axis=1) for line in blocks], axis=0)

    lh, ll, rh, rl = side(left, 0), side(left, 1), side(right, 0), side(right, 1)
    return jnp.dot(
        jnp.concatenate([lh, lh, ll], axis=1), jnp.concatenate([rh, rl, rh], axis=0), preferred_element_type=F32
    )


def get(ref, i, head=0):
    return ref[pl.ds(head + i * B, B), :]


def put(ref, i, block, head=0):
    ref[pl.ds(head + i * B, B), :] = block


class Copies:
    def __init__(self, sems):
        self.sems, self.count = sems, 0

    def start(self, source, target):
        copy = pltpu.make_async_copy(source, target, self.sems.at[self.count])
        self.count += 1
        copy.start()
        return copy


def pack_kernel(x, pat, c1, ea, tw, c2, we, stage, toward, sides, table, sems):
    odd = lax.rem(lax.axis_index("row"), 2)
    dma = Copies(sems)
    table_load = dma.start(pat, table)
    order = (0, 3, 1, 2)
    loads = {}
    for kind in (CR, MID, TW):
        slots = pl.ds(slot(kind, -1, odd), 3)
        for v in order:
            loads[kind, v] = dma.start(x.at[0, v, slots], stage.at[v, slots])
    table_load.wait()
    rows = lax.broadcasted_iota(jnp.int32, (HEAD, B), 0)
    present = jnp.zeros((HEAD, B), F32)
    for v in range(4):
        present = jnp.where(rows == v, weight(table, v, 4), present)
    for ref in (toward, ea, tw):
        ref[pl.ds(0, HEAD), :] = present

    stores = []
    for kind in (CR, MID, TW):
        for v in order:
            loads[kind, v].wait()
            for j in (-1, 0, 1):
                s = slot(kind, j, odd)
                block = stage[v, s] * weight(table, v, s)
                i = at(kind, v, j)
                if kind == CR:
                    put(toward, i, block, HEAD)
                else:
                    put(tw, i - 12, block, HEAD)
                if v == 3 and j >= 0:
                    put(ea, SIDE[kind] + j, block, HEAD)
                if v == 0 and j < 1:
                    put(sides, SIDE[kind] + j + 1, block)
            if kind == TW and v == 0:
                stores.append(dma.start(sides, we))
        if kind == CR:
            stores.append(dma.start(toward, c1))
        if kind == MID:
            stores.append(dma.start(tw.at[pl.ds(HEAD + 12 * B, 12 * B), :], c2))
    for copy in stores:
        copy.wait()


def near_kernel(alpha, beta, c1m, twm, tw, acc, lefts, pairs, few, total, lefts_here, lh, ll, sh, sl, rh, rl, sems):
    dma = Copies(sems)
    stores = []
    def own(kind, v, j):
        i = at(kind, v, j)
        return get(c1m, i, HEAD) if kind == CR else get(twm, i - 12, HEAD)

    sources = {at(CR, v, a): at(CR, v, a) for v in range(4) for a in (-1, 0, 1)}
    sources.update({at(TW, 0, -1): 12, at(TW, 3, 1): 13, at(MID, 0, -1): 14, at(MID, 3, 1): 15})

    def prepare(v):
        for kind in KINDS:
            for j in (-1, 0, 1):
                i = at(kind, v, j)
                block = own(kind, v, j)
                total[v * 9 + kind * 3 + j + 1] = alpha[...] * block
                rh[i], rl[i] = split(block)
                high, low = split(beta[...] * block)
                if kind != CR:
                    lh[i - 12], ll[i - 12] = high, low
                if i in sources:
                    lefts_here[sources[i]], lefts_here[16 + sources[i]] = high, low
        for j in (-1, 0, 1):
            for kind in (TW, MID):
                i = at(kind, v, j) - 12
                sh[i], sl[i] = split(get(tw, i, HEAD))

    left = lambda kind, v, j: (lh[at(kind, v, j) - 12], ll[at(kind, v, j) - 12])
    mine = lambda kind, v, j: (rh[at(kind, v, j)], rl[at(kind, v, j)])
    theirs = lambda kind, v, j: (sh[at(kind, v, j) - 12], sl[at(kind, v, j) - 12])

    def add(kind, v, sv, block):
        total[v * 9 + kind * 3 + sv + 1] += block

    for w in range(4):
        prepare(w)
    stores.append(dma.start(lefts_here, lefts))
    for w in range(4):
        for t in (0, -1, 1):
            targets = [(w - a, a) for a in (-1, 0, 1) if 0 <= w - a < 4 and -1 <= a + t <= 1]
            lines = [[left(MID, v, a), left(TW, v, a)] for v, a in targets]
            right = [[mine(MID, w, t), mine(TW, w, t)], [theirs(TW, w, t), theirs(MID, w, t)]]
            both = dot3(lines, right)
            only = dot3([line[:1] for line in lines], [[mine(CR, w, t)]])
            for n, (v, a) in enumerate(targets):
                rows = slice(n * B, (n + 1) * B)
                add(MID, v, a + t, both[rows, :B])
                add(TW, v, a + t, both[rows, B:])
                add(CR, v, a + t, only[rows])
        for v in range(4):
            if w == min(v + 1, 3):
                stores.append(dma.start(total.at[pl.ds(v * 9, 9)], acc.at[pl.ds(v * 9, 9)]))
    present = lambda v: twm[pl.ds(v, 1), :]
    other = lambda v: tw[pl.ds(v, 1), :]
    listed = []
    for v in range(4):
        listed.append((own(MID, v, 0), mine(MID, v, 0)))
        listed.append((own(TW, v, 0) * present(v), theirs(TW, v, 0)))
    for v in range(3):
        listed.append((own(MID, v, 1) * (present(v) + present(v + 1)), mine(MID, v + 1, -1)))
        listed.append((own(TW, v + 1, -1) * (present(v + 1) + other(v)), theirs(TW, v, 1)))
    value = beta[...] * dot3([[split(a) for a, _ in listed]], [[b] for _, b in listed])
    for v in range(4):
        value += alpha[...] * own(MID, v, 0)
    pairs[...] = value
    few[pl.ds(0, HEAD), :] = twm[pl.ds(0, HEAD), :]
    few[pl.ds(HEAD, HEAD), :] = tw[pl.ds(0, HEAD), :]
    kept = [own(CR, v, 0) for v in range(4)] + [own(CR, v, -1) for v in (1, 2, 3)] + [own(MID, 0, -1), get(tw, 0, HEAD)]
    for i, block in enumerate(kept):
        put(few, i, block, 2 * HEAD)
    for copy in stores:
        copy.wait()


def middle_kernel(beta, pairs, few, c1, ea, we, cc, tc, shares):
    for out, kind, head in ((cc, CR, 0), (tc, MID, 0)):
        for i in range(4):
            put(out, i, get(ea, SIDE[kind] + i, HEAD), head)
            put(out, 4 + i, get(we, SIDE[kind] + i), head)
    own = lambda v: few[pl.ds(v, 1), :]
    far = lambda v: c1[pl.ds(v, 1), :]
    west = ea[pl.ds(3, 1), :]
    kept = lambda i: get(few, i, 2 * HEAD)
    listed = []
    for v in range(4):
        listed.append((own(v), kept(v), get(c1, at(CR, v, 0), HEAD)))
    for v in range(3):
        listed.append((own(v + 1) + far(v), kept(4 + v), get(c1, at(CR, v, 1), HEAD)))
    listed.append((west + own(0), get(ea, SIDE[MID] + 1, HEAD), kept(7)))
    listed.append((west + far(0), get(ea, SIDE[CR] + 1, HEAD), get(c1, 0, HEAD)))
    listed.append((west + few[pl.ds(HEAD, 1), :], get(ea, SIDE[TW] + 1, HEAD), kept(8)))
    value = pairs[...] + beta[...] * dot3([[split(a * w) for w, a, _ in listed]], [[split(b)] for _, _, b in listed])
    rows = lax.broadcasted_iota(jnp.int32, (B, B), 0)
    columns = lax.broadcasted_iota(jnp.int32, (B, B), 1)
    line = jnp.sum(jnp.where(rows == columns, value, 0.0), axis=0, keepdims=True)
    shares[...] = jnp.broadcast_to(line, (B, B))


def sum_kernel(scale, shares, after, out):
    out[0, 0] = jnp.sum(shares[...]) * scale


def final_kernel(pat, lefts, acc, c1, c2, ea, we, cc, tc, out, total, stage, sems):
    odd = lax.rem(lax.axis_index("row"), 2)
    dma = Copies(sems)
    left = lambda i: (lefts[i], lefts[16 + i])
    seen = set()

    def add(kind, v, sv, block):
        i = v * 9 + kind * 3 + sv + 1
        total[i] = (total[i] if i in seen else acc[i]) + block
        seen.add(i)

    def spread(source, rights, places):
        result = dot3([[left(source)]], [[split(block) for block in rights]])
        for n, (kind, v, sv) in enumerate(places):
            add(kind, v, sv, result[:, n * B : (n + 1) * B])

    spread(14, [get(ea, i, HEAD) for i in range(6)], [(k, 0, s) for k in SIDE for s in (-1, 0)])
    spread(15, [get(we, i) for i in range(6)], [(k, 3, s) for k in SIDE for s in (0, 1)])
    spread(12, [get(tc, i) for i in range(4)], [(TW, 0, -1), (TW, 0, 0), (MID, 0, -1), (MID, 0, 0)])
    spread(13, [get(tc, 4 + i) for i in range(4)], [(TW, 3, 0), (TW, 3, 1), (MID, 3, 0), (MID, 3, 1)])
    spread(at(CR, 0, -1), [get(cc, i) for i in range(4)], [(MID, 0, -1), (MID, 0, 0), (CR, 0, -1), (CR, 0, 0)])
    spread(at(CR, 3, 1), [get(cc, 4 + i) for i in range(4)], [(MID, 3, 0), (MID, 3, 1), (CR, 3, 0), (CR, 3, 1)])

    stores = []

    def finish(v):
        for kind in KINDS:
            for sv in (-1, 0, 1):
                i, s = v * 9 + kind * 3 + sv + 1, slot(kind, sv, odd)
                stage[v, s] = weight(pat, v, s) * (total[i] if i in seen else acc[i])
        stores.append(dma.start(stage.at[v], out.at[0, v]))

    for w in range(4):
        for t in (0, -1, 1):
            targets = [(w - a, a) for a in (-1, 0, 1) if 0 <= w - a < 4 and -1 <= a + t <= 1]
            lines = [[left(at(CR, v, a))] for v, a in targets]
            result = dot3(lines, [[split(get(c1, at(CR, w, t), HEAD)), split(get(c2, at(CR, w, t)))]])
            for n, (v, a) in enumerate(targets):
                rows = slice(n * B, (n + 1) * B)
                add(MID, v, a + t, result[rows, :B])
                add(CR, v, a + t, result[rows, B:])
        if w >= 1:
            finish(w - 1)
    finish(3)
    for copy in stores:
        copy.wait()


def body(x, pat, alpha, beta):
    rows, columns = lax.axis_size("row"), lax.axis_size("col")

    def moved(message, step):
        pairs = []
        for r in range(rows):
            for c in range(columns):
                r2, c2 = step(r, c)
                pairs.append((r * columns + c, (r2 % rows) * columns + c2 % columns))
        return lax.ppermute(message, AXES, pairs)

    def call(kernel, outs, args, specs, size, scratch=()):
        spaces = [pltpu.HBM if s is ANY or a is pat else None for a, s in zip(args, specs)]
        return pl.pallas_call(
            kernel,
            out_shape=[pltpu.HBM(o.shape, o.dtype) if s is ANY or s is FAR else o for o, s in outs],
            in_specs=specs,
            out_specs=[VMEM if s is FAR else s for _, s in outs],
            scratch_shapes=scratch,
            compiler_params=pltpu.CompilerParams(vmem_limit_bytes=size * 1024 * 1024),
            cost_estimate=pl.CostEstimate(flops=1000, bytes_accessed=1000, transcendentals=0),
        )(*[pltpu.with_memory_space_constraint(a, m) if m else a for a, m in zip(args, spaces)])

    shape = lambda *dims, dtype=F32: jax.ShapeDtypeStruct(dims, dtype)
    lines = lambda count, head=0: shape(count * B + head, B)
    sems = lambda count: pltpu.SemaphoreType.DMA((count,))
    far = lambda a: pltpu.with_memory_space_constraint(a, pltpu.HBM)
    vmem = lambda *dims, dtype=F32: pltpu.VMEM(dims, dtype)
    crossing = lambda r: r - 1 if r % 2 == 0 else r + 1
    cross = lambda r, c: (crossing(r), c)
    twin = lambda r, c: (r ^ 1, c)
    east = lambda r, c: (r, c + 1)
    west = lambda r, c: (r, c - 1)
    alpha, beta = alpha.reshape(1, 1), beta.reshape(1, 1)

    messages = call(
        pack_kernel,
        [(lines(12, HEAD), ANY), (lines(6, HEAD), VMEM), (lines(24, HEAD), VMEM), (lines(12), ANY), (lines(6), ANY)],
        (x, pat),
        [ANY, ANY],
        10,
        [vmem(4, 9, B, B), vmem(12 * B + HEAD, B), vmem(6 * B, B), pltpu.SMEM(pat.shape, jnp.int32), sems(16)],
    )
    c1, ea, tw, c2, we = [moved(m, s) for m, s in zip(messages, [cross, east, twin, cross, west])]
    c1m, _, twm = messages[:3]
    acc, lefts, pairs, few = call(
        near_kernel,
        [(shape(36, B, B), ANY), (shape(32, B, B, dtype=BF16), ANY), (shape(B, B), VMEM), (lines(9, 2 * HEAD), VMEM)],
        (alpha, beta, far(c1m), twm, tw),
        [VMEM] * 5,
        14,
        [vmem(36, B, B)] + [vmem(n, B, B, dtype=BF16) for n in (32, 24, 24, 24, 24, 36, 36)] + [sems(5)],
    )
    *corners, shares = call(
        middle_kernel,
        [(lines(8), VMEM), (lines(8), VMEM), (shape(B, B), VMEM)],
        (beta, pairs, few, c1, ea, we),
        [VMEM] * 6,
        4,
    )
    cc, tc = moved(corners[0], cross), moved(corners[1], twin)
    gathered = lax.all_to_all(shares, AXES, 0, 0)
    (updated,) = call(
        final_kernel,
        [(shape(*x.shape), ANY)],
        (pat, far(lefts), far(acc), c1, c2, ea, we, cc, tc),
        [SMEM] + [VMEM] * 8,
        14,
        [vmem(36, B, B), vmem(4, 9, B, B), sems(4)],
    )
    scale = 1.0 / (rows * columns * x.shape[1])
    (trace,) = call(functools.partial(sum_kernel, scale), [(shape(1, 1), SMEM)], (gathered, updated), [VMEM, ANY], 2)
    return (updated, trace.reshape(()))


def solution(mesh):
    placed = (P("row", "col", None, None, None), P("row", "col", None), P(), P())
    return jax.shard_map(
        body,
        mesh=mesh,
        in_specs=placed,
        out_specs=(P("row", "col", None, None, None), P()),
        check_vma=False,
    )
```

```python
import functools

import jax
import jax.numpy as jnp
from jax import lax
from jax.experimental import pallas as pl
from jax.experimental.pallas import tpu as pltpu
from jax.sharding import PartitionSpec as P

CR, TW, MID = KINDS = (0, 1, 2)
AXES = ("row", "col")
B = 128
F32 = jnp.float32
BF16 = jnp.bfloat16
ANY = pl.BlockSpec(memory_space=pl.ANY)
VMEM = pl.BlockSpec(memory_space=pltpu.VMEM)
FAR = None
SMEM = pl.BlockSpec(memory_space=pltpu.SMEM)


def at(kind, v, j):
    return kind * 12 + v * 3 + j + 1


SIDE = {CR: 0, MID: 2, TW: 4}
HEAD = 8


def slot(kind, dv, odd):
    base = {CR: 6 * odd, MID: 3, TW: 6 - 6 * odd}[kind]
    return base + dv + 1


def weight(pat, v, s):
    return pat[0, v, s].astype(F32)


def split(block):
    high = block.astype(BF16)
    return high, (block - high.astype(F32)).astype(BF16)


def dot3(left, right):
    def side(blocks, part):
        return jnp.concatenate([jnp.concatenate([b[part] for b in line], axis=1) for line in blocks], axis=0)

    lh, ll, rh, rl = side(left, 0), side(left, 1), side(right, 0), side(right, 1)
    return jnp.dot(
        jnp.concatenate([lh, lh, ll], axis=1), jnp.concatenate([rh, rl, rh], axis=0), preferred_element_type=F32
    )


def get(ref, i, head=0):
    return ref[pl.ds(head + i * B, B), :]


def put(ref, i, block, head=0):
    ref[pl.ds(head + i * B, B), :] = block


class Copies:
    def __init__(self, sems):
        self.sems, self.count = sems, 0

    def start(self, source, target):
        copy = pltpu.make_async_copy(source, target, self.sems.at[self.count])
        self.count += 1
        copy.start()
        return copy


def pack_kernel(x, pat, c1, ea, tw, c2, we, stage, toward, sides, table, sems):
    odd = lax.rem(lax.axis_index("row"), 2)
    dma = Copies(sems)
    table_load = dma.start(pat, table)
    order = (0, 3, 1, 2)
    loads = {}
    for kind in (CR, MID, TW):
        slots = pl.ds(slot(kind, -1, odd), 3)
        for v in order:
            loads[kind, v] = dma.start(x.at[0, v, slots], stage.at[v, slots])
    table_load.wait()
    rows = lax.broadcasted_iota(jnp.int32, (HEAD, B), 0)
    present = jnp.zeros((HEAD, B), F32)
    for v in range(4):
        present = jnp.where(rows == v, weight(table, v, 4), present)
    for ref in (toward, ea, tw):
        ref[pl.ds(0, HEAD), :] = present

    stores = []
    for kind in (CR, MID, TW):
        for v in order:
            loads[kind, v].wait()
            for j in (-1, 0, 1):
                s = slot(kind, j, odd)
                block = stage[v, s] * weight(table, v, s)
                i = at(kind, v, j)
                if kind == CR:
                    put(toward, i, block, HEAD)
                else:
                    put(tw, i - 12, block, HEAD)
                if v == 3 and j >= 0:
                    put(ea, SIDE[kind] + j, block, HEAD)
                if v == 0 and j < 1:
                    put(sides, SIDE[kind] + j + 1, block)
            if kind == TW and v == 0:
                stores.append(dma.start(sides, we))
        if kind == CR:
            stores.append(dma.start(toward, c1))
        if kind == MID:
            stores.append(dma.start(tw.at[pl.ds(HEAD + 12 * B, 12 * B), :], c2))
    for copy in stores:
        copy.wait()


def near_kernel(alpha, beta, c1m, twm, tw, acc, lefts, pairs, few, total, lefts_here, lh, ll, sh, sl, rh, rl, sems):
    dma = Copies(sems)
    stores = []
    def own(kind, v, j):
        i = at(kind, v, j)
        return get(c1m, i, HEAD) if kind == CR else get(twm, i - 12, HEAD)

    sources = {at(CR, v, a): at(CR, v, a) for v in range(4) for a in (-1, 0, 1)}
    sources.update({at(TW, 0, -1): 12, at(TW, 3, 1): 13, at(MID, 0, -1): 14, at(MID, 3, 1): 15})

    def prepare(v):
        for kind in KINDS:
            for j in (-1, 0, 1):
                i = at(kind, v, j)
                block = own(kind, v, j)
                total[v * 9 + kind * 3 + j + 1] = alpha[()] * block
                rh[i], rl[i] = split(block)
                high, low = split(beta[()] * block)
                if kind != CR:
                    lh[i - 12], ll[i - 12] = high, low
                if i in sources:
                    lefts_here[sources[i]], lefts_here[16 + sources[i]] = high, low
        for j in (-1, 0, 1):
            for kind in (TW, MID):
                i = at(kind, v, j) - 12
                sh[i], sl[i] = split(get(tw, i, HEAD))

    left = lambda kind, v, j: (lh[at(kind, v, j) - 12], ll[at(kind, v, j) - 12])
    mine = lambda kind, v, j: (rh[at(kind, v, j)], rl[at(kind, v, j)])
    theirs = lambda kind, v, j: (sh[at(kind, v, j) - 12], sl[at(kind, v, j) - 12])

    def add(kind, v, sv, block):
        total[v * 9 + kind * 3 + sv + 1] += block

    for w in range(4):
        prepare(w)
    stores.append(dma.start(lefts_here, lefts))
    for w in range(4):
        for t in (0, -1, 1):
            targets = [(w - a, a) for a in (-1, 0, 1) if 0 <= w - a < 4 and -1 <= a + t <= 1]
            lines = [[left(MID, v, a), left(TW, v, a)] for v, a in targets]
            right = [[mine(MID, w, t), mine(TW, w, t)], [theirs(TW, w, t), theirs(MID, w, t)]]
            both = dot3(lines, right)
            only = dot3([line[:1] for line in lines], [[mine(CR, w, t)]])
            for n, (v, a) in enumerate(targets):
                rows = slice(n * B, (n + 1) * B)
                add(MID, v, a + t, both[rows, :B])
                add(TW, v, a + t, both[rows, B:])
                add(CR, v, a + t, only[rows])
        for v in range(4):
            if w == min(v + 1, 3):
                stores.append(dma.start(total.at[pl.ds(v * 9, 9)], acc.at[pl.ds(v * 9, 9)]))
    present = lambda v: twm[pl.ds(v, 1), :]
    other = lambda v: tw[pl.ds(v, 1), :]
    listed = []
    for v in range(4):
        listed.append((own(MID, v, 0), mine(MID, v, 0)))
        listed.append((own(TW, v, 0) * present(v), theirs(TW, v, 0)))
    for v in range(3):
        listed.append((own(MID, v, 1) * (present(v) + present(v + 1)), mine(MID, v + 1, -1)))
        listed.append((own(TW, v + 1, -1) * (present(v + 1) + other(v)), theirs(TW, v, 1)))
    value = beta[()] * dot3([[split(a) for a, _ in listed]], [[b] for _, b in listed])
    for v in range(4):
        value += alpha[()] * own(MID, v, 0)
    pairs[...] = value
    few[pl.ds(0, HEAD), :] = twm[pl.ds(0, HEAD), :]
    few[pl.ds(HEAD, HEAD), :] = tw[pl.ds(0, HEAD), :]
    kept = [own(CR, v, 0) for v in range(4)] + [own(CR, v, -1) for v in (1, 2, 3)] + [own(MID, 0, -1), get(tw, 0, HEAD)]
    for i, block in enumerate(kept):
        put(few, i, block, 2 * HEAD)
    for copy in stores:
        copy.wait()


def middle_kernel(beta, pairs, few, c1, ea, we, cc, tc, shares):
    for out, kind, head in ((cc, CR, 0), (tc, MID, 0)):
        for i in range(4):
            put(out, i, get(ea, SIDE[kind] + i, HEAD), head)
            put(out, 4 + i, get(we, SIDE[kind] + i), head)
    own = lambda v: few[pl.ds(v, 1), :]
    far = lambda v: c1[pl.ds(v, 1), :]
    west = ea[pl.ds(3, 1), :]
    kept = lambda i: get(few, i, 2 * HEAD)
    listed = []
    for v in range(4):
        listed.append((own(v), kept(v), get(c1, at(CR, v, 0), HEAD)))
    for v in range(3):
        listed.append((own(v + 1) + far(v), kept(4 + v), get(c1, at(CR, v, 1), HEAD)))
    listed.append((west + own(0), get(ea, SIDE[MID] + 1, HEAD), kept(7)))
    listed.append((west + far(0), get(ea, SIDE[CR] + 1, HEAD), get(c1, 0, HEAD)))
    listed.append((west + few[pl.ds(HEAD, 1), :], get(ea, SIDE[TW] + 1, HEAD), kept(8)))
    value = pairs[...] + beta[()] * dot3([[split(a * w) for w, a, _ in listed]], [[split(b)] for _, _, b in listed])
    rows = lax.broadcasted_iota(jnp.int32, (B, B), 0)
    columns = lax.broadcasted_iota(jnp.int32, (B, B), 1)
    line = jnp.sum(jnp.where(rows == columns, value, 0.0), axis=0, keepdims=True)
    shares[...] = jnp.broadcast_to(line, (B, B))


def sum_kernel(scale, shares, after, out):
    out[0, 0] = jnp.sum(shares[...]) * scale


def final_kernel(pat, lefts, acc, c1, c2, ea, we, cc, tc, out, total, stage, sems):
    odd = lax.rem(lax.axis_index("row"), 2)
    dma = Copies(sems)
    left = lambda i: (lefts[i], lefts[16 + i])
    seen = set()

    def add(kind, v, sv, block):
        i = v * 9 + kind * 3 + sv + 1
        total[i] = (total[i] if i in seen else acc[i]) + block
        seen.add(i)

    def spread(source, rights, places):
        result = dot3([[left(source)]], [[split(block) for block in rights]])
        for n, (kind, v, sv) in enumerate(places):
            add(kind, v, sv, result[:, n * B : (n + 1) * B])

    spread(14, [get(ea, i, HEAD) for i in range(6)], [(k, 0, s) for k in SIDE for s in (-1, 0)])
    spread(15, [get(we, i) for i in range(6)], [(k, 3, s) for k in SIDE for s in (0, 1)])
    spread(12, [get(tc, i) for i in range(4)], [(TW, 0, -1), (TW, 0, 0), (MID, 0, -1), (MID, 0, 0)])
    spread(13, [get(tc, 4 + i) for i in range(4)], [(TW, 3, 0), (TW, 3, 1), (MID, 3, 0), (MID, 3, 1)])
    spread(at(CR, 0, -1), [get(cc, i) for i in range(4)], [(MID, 0, -1), (MID, 0, 0), (CR, 0, -1), (CR, 0, 0)])
    spread(at(CR, 3, 1), [get(cc, 4 + i) for i in range(4)], [(MID, 3, 0), (MID, 3, 1), (CR, 3, 0), (CR, 3, 1)])

    stores = []

    def finish(v):
        for kind in KINDS:
            for sv in (-1, 0, 1):
                i, s = v * 9 + kind * 3 + sv + 1, slot(kind, sv, odd)
                stage[v, s] = weight(pat, v, s) * (total[i] if i in seen else acc[i])
        stores.append(dma.start(stage.at[v], out.at[0, v]))

    for w in range(4):
        for t in (0, -1, 1):
            targets = [(w - a, a) for a in (-1, 0, 1) if 0 <= w - a < 4 and -1 <= a + t <= 1]
            lines = [[left(at(CR, v, a))] for v, a in targets]
            result = dot3(lines, [[split(get(c1, at(CR, w, t), HEAD)), split(get(c2, at(CR, w, t)))]])
            for n, (v, a) in enumerate(targets):
                rows = slice(n * B, (n + 1) * B)
                add(MID, v, a + t, result[rows, :B])
                add(CR, v, a + t, result[rows, B:])
        if w >= 1:
            finish(w - 1)
    finish(3)
    for copy in stores:
        copy.wait()


def body(x, pat, alpha, beta):
    rows, columns = lax.axis_size("row"), lax.axis_size("col")

    def moved(message, step):
        pairs = []
        for r in range(rows):
            for c in range(columns):
                r2, c2 = step(r, c)
                pairs.append((r * columns + c, (r2 % rows) * columns + c2 % columns))
        return lax.ppermute(message, AXES, pairs)

    def call(kernel, outs, args, specs, size, scratch=()):
        spaces = [pltpu.HBM if s is ANY or a is pat else None for a, s in zip(args, specs)]
        return pl.pallas_call(
            kernel,
            out_shape=[pltpu.HBM(o.shape, o.dtype) if s is ANY or s is FAR else o for o, s in outs],
            in_specs=specs,
            out_specs=[VMEM if s is FAR else s for _, s in outs],
            scratch_shapes=scratch,
            compiler_params=pltpu.CompilerParams(vmem_limit_bytes=size * 1024 * 1024),
            cost_estimate=pl.CostEstimate(flops=1000, bytes_accessed=1000, transcendentals=0),
        )(*[pltpu.with_memory_space_constraint(a, m) if m else a for a, m in zip(args, spaces)])

    shape = lambda *dims, dtype=F32: jax.ShapeDtypeStruct(dims, dtype)
    lines = lambda count, head=0: shape(count * B + head, B)
    sems = lambda count: pltpu.SemaphoreType.DMA((count,))
    far = lambda a: pltpu.with_memory_space_constraint(a, pltpu.HBM)
    vmem = lambda *dims, dtype=F32: pltpu.VMEM(dims, dtype)
    crossing = lambda r: r - 1 if r % 2 == 0 else r + 1
    cross = lambda r, c: (crossing(r), c)
    twin = lambda r, c: (r ^ 1, c)
    east = lambda r, c: (r, c + 1)
    west = lambda r, c: (r, c - 1)

    messages = call(
        pack_kernel,
        [(lines(12, HEAD), ANY), (lines(6, HEAD), VMEM), (lines(24, HEAD), VMEM), (lines(12), ANY), (lines(6), ANY)],
        (x, pat),
        [ANY, ANY],
        10,
        [vmem(4, 9, B, B), vmem(12 * B + HEAD, B), vmem(6 * B, B), pltpu.SMEM(pat.shape, jnp.int32), sems(16)],
    )
    c1, ea, tw, c2, we = [moved(m, s) for m, s in zip(messages, [cross, east, twin, cross, west])]
    c1m, _, twm = messages[:3]
    acc, lefts, pairs, few = call(
        near_kernel,
        [(shape(36, B, B), ANY), (shape(32, B, B, dtype=BF16), ANY), (shape(B, B), VMEM), (lines(9, 2 * HEAD), VMEM)],
        (alpha, beta, far(c1m), twm, tw),
        [SMEM, SMEM] + [VMEM] * 3,
        14,
        [vmem(36, B, B)] + [vmem(n, B, B, dtype=BF16) for n in (32, 24, 24, 24, 24, 36, 36)] + [sems(5)],
    )
    *corners, shares = call(
        middle_kernel,
        [(lines(8), VMEM), (lines(8), VMEM), (shape(B, B), VMEM)],
        (beta, pairs, few, c1, ea, we),
        [SMEM] + [VMEM] * 5,
        4,
    )
    cc, tc = moved(corners[0], cross), moved(corners[1], twin)
    gathered = lax.all_to_all(shares, AXES, 0, 0)
    (updated,) = call(
        final_kernel,
        [(shape(*x.shape), ANY)],
        (pat, far(lefts), far(acc), c1, c2, ea, we, cc, tc),
        [SMEM] + [VMEM] * 8,
        14,
        [vmem(36, B, B), vmem(4, 9, B, B), sems(4)],
    )
    scale = 1.0 / (rows * columns * x.shape[1])
    (trace,) = call(functools.partial(sum_kernel, scale), [(shape(1, 1), SMEM)], (gathered, updated), [VMEM, ANY], 2)
    return (updated, trace.reshape(()))


def solution(mesh):
    placed = (P("row", "col", None, None, None), P("row", "col", None), P(), P())
    return jax.shard_map(
        body,
        mesh=mesh,
        in_specs=placed,
        out_specs=(P("row", "col", None, None, None), P()),
        check_vma=False,
    )
```

```python
import functools

import jax
import jax.numpy as jnp
from jax import lax
from jax.experimental import pallas as pl
from jax.experimental.pallas import tpu as pltpu
from jax.sharding import PartitionSpec as P

CR, TW, MID = KINDS = (0, 1, 2)
AXES = ("row", "col")
B = 128
F32 = jnp.float32
BF16 = jnp.bfloat16
ANY = pl.BlockSpec(memory_space=pl.ANY)
VMEM = pl.BlockSpec(memory_space=pltpu.VMEM)
FAR = None
SMEM = pl.BlockSpec(memory_space=pltpu.SMEM)


def at(kind, v, j):
    return kind * 12 + v * 3 + j + 1


SIDE = {CR: 0, MID: 2, TW: 4}
HEAD = 8


def slot(kind, dv, odd):
    base = {CR: 6 * odd, MID: 3, TW: 6 - 6 * odd}[kind]
    return base + dv + 1


def weight(pat, v, s):
    return pat[0, v, s].astype(F32)


def split(block):
    high = block.astype(BF16)
    return high, (block - high.astype(F32)).astype(BF16)


def dot3(left, right):
    def side(blocks, part):
        return jnp.concatenate([jnp.concatenate([b[part] for b in line], axis=1) for line in blocks], axis=0)

    lh, ll, rh, rl = side(left, 0), side(left, 1), side(right, 0), side(right, 1)
    return jnp.dot(
        jnp.concatenate([lh, lh, ll], axis=1), jnp.concatenate([rh, rl, rh], axis=0), preferred_element_type=F32
    )


def get(ref, i, head=0):
    return ref[pl.ds(head + i * B, B), :]


def put(ref, i, block, head=0):
    ref[pl.ds(head + i * B, B), :] = block


class Copies:
    def __init__(self, sems):
        self.sems, self.count = sems, 0

    def start(self, source, target):
        copy = pltpu.make_async_copy(source, target, self.sems.at[self.count])
        self.count += 1
        copy.start()
        return copy


def pack_kernel(x, pat, c1, ea, tw, c2, we, stage, toward, westward, table, sems):
    odd = lax.rem(lax.axis_index("row"), 2)
    dma = Copies(sems)
    table_load = dma.start(pat, table)
    order = (0, 3, 1, 2)
    loads = {}
    for kind in (CR, MID, TW):
        slots = pl.ds(slot(kind, -1, odd), 3)
        for v in order:
            loads[kind, v] = dma.start(x.at[0, v, slots], stage.at[v, slots])
    table_load.wait()
    rows = lax.broadcasted_iota(jnp.int32, (HEAD, B), 0)
    present = jnp.zeros((HEAD, B), F32)
    for v in range(4):
        present = jnp.where(rows == v, weight(table, v, 4), present)
    for ref in (toward, ea, tw):
        ref[pl.ds(0, HEAD), :] = present

    stores = []
    for kind in (CR, MID, TW):
        for v in order:
            loads[kind, v].wait()
            for j in (-1, 0, 1):
                s = slot(kind, j, odd)
                block = stage[v, s] * weight(table, v, s)
                i = at(kind, v, j)
                if kind == CR:
                    put(toward, i, block, HEAD)
                else:
                    put(tw, i - 12, block, HEAD)
                if v == 3 and j >= 0:
                    put(ea, SIDE[kind] + j, block, HEAD)
                if v == 0 and j < 1:
                    put(westward, SIDE[kind] + j + 1, block)
            if kind == TW and v == 0:
                stores.append(dma.start(westward, we))
        if kind == CR:
            stores.append(dma.start(toward, c1))
        if kind == MID:
            stores.append(dma.start(tw.at[pl.ds(HEAD + 12 * B, 12 * B), :], c2))
    for copy in stores:
        copy.wait()


def near_kernel(alpha, beta, c1m, twm, tw, acc, lefts, pairs, few, total, lefts_here, lh, ll, sh, sl, rh, rl, sems):
    dma = Copies(sems)
    stores = []
    def own(kind, v, j):
        i = at(kind, v, j)
        return get(c1m, i, HEAD) if kind == CR else get(twm, i - 12, HEAD)

    sources = {at(CR, v, a): at(CR, v, a) for v in range(4) for a in (-1, 0, 1)}
    sources.update({at(TW, 0, -1): 12, at(TW, 3, 1): 13, at(MID, 0, -1): 14, at(MID, 3, 1): 15})

    def prepare(v):
        for kind in KINDS:
            for j in (-1, 0, 1):
                i = at(kind, v, j)
                block = own(kind, v, j)
                total[v * 9 + kind * 3 + j + 1] = alpha[()] * block
                rh[i], rl[i] = split(block)
                high, low = split(beta[()] * block)
                if kind != CR:
                    lh[i - 12], ll[i - 12] = high, low
                if i in sources:
                    lefts_here[sources[i]], lefts_here[16 + sources[i]] = high, low
        for j in (-1, 0, 1):
            for kind in (TW, MID):
                i = at(kind, v, j) - 12
                sh[i], sl[i] = split(get(tw, i, HEAD))

    left = lambda kind, v, j: (lh[at(kind, v, j) - 12], ll[at(kind, v, j) - 12])
    mine = lambda kind, v, j: (rh[at(kind, v, j)], rl[at(kind, v, j)])
    theirs = lambda kind, v, j: (sh[at(kind, v, j) - 12], sl[at(kind, v, j) - 12])

    def add(kind, v, sv, block):
        total[v * 9 + kind * 3 + sv + 1] += block

    for w in range(4):
        prepare(w)
    stores.append(dma.start(lefts_here, lefts))
    for w in range(4):
        for t in (0, -1, 1):
            targets = [(w - a, a) for a in (-1, 0, 1) if 0 <= w - a < 4 and -1 <= a + t <= 1]
            lines = [[left(MID, v, a), left(TW, v, a)] for v, a in targets]
            right = [[mine(MID, w, t), mine(TW, w, t)], [theirs(TW, w, t), theirs(MID, w, t)]]
            both = dot3(lines, right)
            only = dot3([line[:1] for line in lines], [[mine(CR, w, t)]])
            for n, (v, a) in enumerate(targets):
                rows = slice(n * B, (n + 1) * B)
                add(MID, v, a + t, both[rows, :B])
                add(TW, v, a + t, both[rows, B:])
                add(CR, v, a + t, only[rows])
        for v in range(4):
            if w == min(v + 1, 3):
                stores.append(dma.start(total.at[pl.ds(v * 9, 9)], acc.at[pl.ds(v * 9, 9)]))
    present = lambda v: twm[pl.ds(v, 1), :]
    other = lambda v: tw[pl.ds(v, 1), :]
    listed = []
    for v in range(4):
        listed.append((own(MID, v, 0), mine(MID, v, 0)))
        listed.append((own(TW, v, 0) * present(v), theirs(TW, v, 0)))
    for v in range(3):
        listed.append((own(MID, v, 1) * (present(v) + present(v + 1)), mine(MID, v + 1, -1)))
        listed.append((own(TW, v + 1, -1) * (present(v + 1) + other(v)), theirs(TW, v, 1)))
    value = beta[()] * dot3([[split(a) for a, _ in listed]], [[b] for _, b in listed])
    for v in range(4):
        value += alpha[()] * own(MID, v, 0)
    pairs[...] = value
    few[pl.ds(0, HEAD), :] = twm[pl.ds(0, HEAD), :]
    few[pl.ds(HEAD, HEAD), :] = tw[pl.ds(0, HEAD), :]
    kept = [own(CR, v, 0) for v in range(4)] + [own(CR, v, -1) for v in (1, 2, 3)] + [own(MID, 0, -1), get(tw, 0, HEAD)]
    for i, block in enumerate(kept):
        put(few, i, block, 2 * HEAD)
    for copy in stores:
        copy.wait()


def middle_kernel(beta, pairs, few, c1, ea, we, cc, tc, shares, lines, sem):
    own = lambda v: few[pl.ds(v, 1), :]
    far = lambda v: c1[pl.ds(v, 1), :]
    west = ea[pl.ds(3, 1), :]
    kept = lambda i: get(few, i, 2 * HEAD)
    listed = []
    for v in range(4):
        listed.append((own(v), kept(v), get(c1, at(CR, v, 0), HEAD)))
    for v in range(3):
        listed.append((own(v + 1) + far(v), kept(4 + v), get(c1, at(CR, v, 1), HEAD)))
    listed.append((west + own(0), get(ea, SIDE[MID] + 1, HEAD), kept(7)))
    listed.append((west + far(0), get(ea, SIDE[CR] + 1, HEAD), get(c1, 0, HEAD)))
    listed.append((west + few[pl.ds(HEAD, 1), :], get(ea, SIDE[TW] + 1, HEAD), kept(8)))
    value = pairs[...] + beta[()] * dot3([[split(a * w) for w, a, _ in listed]], [[split(b)] for _, _, b in listed])
    rows = lax.broadcasted_iota(jnp.int32, (B, B), 0)
    columns = lax.broadcasted_iota(jnp.int32, (B, B), 1)
    line = jnp.sum(jnp.where(rows == columns, value, 0.0), axis=0, keepdims=True)
    lines[...] = jnp.broadcast_to(line, (B, B))
    copy = pltpu.make_async_copy(lines, shares, sem)
    copy.start()
    for out, kind in ((cc, CR), (tc, MID)):
        for i in range(4):
            put(out, i, get(ea, SIDE[kind] + i, HEAD))
            put(out, 4 + i, get(we, SIDE[kind] + i))
    copy.wait()


def sum_kernel(scale, shares, after, out):
    out[0, 0] = jnp.sum(shares[...]) * scale


def final_kernel(pat, lefts, acc, c1, c2, ccm, tcm, cc, tc, out, total, stage, sems):
    odd = lax.rem(lax.axis_index("row"), 2)
    dma = Copies(sems)
    left = lambda i: (lefts[i], lefts[16 + i])
    seen = set()

    def add(kind, v, sv, block):
        i = v * 9 + kind * 3 + sv + 1
        total[i] = (total[i] if i in seen else acc[i]) + block
        seen.add(i)

    def spread(source, rights, places):
        result = dot3([[left(source)]], [[split(block) for block in rights]])
        for n, (kind, v, sv) in enumerate(places):
            add(kind, v, sv, result[:, n * B : (n + 1) * B])

    spread(14, [get(ccm, i) for i in range(4)] + [get(tcm, i) for i in (2, 3)], [(k, 0, s) for k in SIDE for s in (-1, 0)])
    spread(15, [get(ccm, 4 + i) for i in range(4)] + [get(tcm, i) for i in (6, 7)], [(k, 3, s) for k in SIDE for s in (0, 1)])
    spread(12, [get(tc, i) for i in range(4)], [(TW, 0, -1), (TW, 0, 0), (MID, 0, -1), (MID, 0, 0)])
    spread(13, [get(tc, 4 + i) for i in range(4)], [(TW, 3, 0), (TW, 3, 1), (MID, 3, 0), (MID, 3, 1)])
    spread(at(CR, 0, -1), [get(cc, i) for i in range(4)], [(MID, 0, -1), (MID, 0, 0), (CR, 0, -1), (CR, 0, 0)])
    spread(at(CR, 3, 1), [get(cc, 4 + i) for i in range(4)], [(MID, 3, 0), (MID, 3, 1), (CR, 3, 0), (CR, 3, 1)])

    stores = []

    def finish(v):
        for kind in KINDS:
            for sv in (-1, 0, 1):
                i, s = v * 9 + kind * 3 + sv + 1, slot(kind, sv, odd)
                stage[v, s] = weight(pat, v, s) * (total[i] if i in seen else acc[i])
        stores.append(dma.start(stage.at[v], out.at[0, v]))

    for w in range(4):
        for t in (0, -1, 1):
            targets = [(w - a, a) for a in (-1, 0, 1) if 0 <= w - a < 4 and -1 <= a + t <= 1]
            lines = [[left(at(CR, v, a))] for v, a in targets]
            result = dot3(lines, [[split(get(c1, at(CR, w, t), HEAD)), split(get(c2, at(CR, w, t)))]])
            for n, (v, a) in enumerate(targets):
                rows = slice(n * B, (n + 1) * B)
                add(MID, v, a + t, result[rows, :B])
                add(CR, v, a + t, result[rows, B:])
        if w >= 1:
            finish(w - 1)
    finish(3)
    for copy in stores:
        copy.wait()


def body(x, pat, alpha, beta):
    rows, columns = lax.axis_size("row"), lax.axis_size("col")

    def moved(message, step):
        pairs = []
        for r in range(rows):
            for c in range(columns):
                r2, c2 = step(r, c)
                pairs.append((r * columns + c, (r2 % rows) * columns + c2 % columns))
        return lax.ppermute(message, AXES, pairs)

    def call(kernel, outs, args, specs, size, scratch=()):
        spaces = [pltpu.HBM if s is ANY or a is pat else None for a, s in zip(args, specs)]
        return pl.pallas_call(
            kernel,
            out_shape=[pltpu.HBM(o.shape, o.dtype) if s is ANY or s is FAR else o for o, s in outs],
            in_specs=specs,
            out_specs=[VMEM if s is FAR else s for _, s in outs],
            scratch_shapes=scratch,
            compiler_params=pltpu.CompilerParams(vmem_limit_bytes=size * 1024 * 1024),
            cost_estimate=pl.CostEstimate(flops=1000, bytes_accessed=1000, transcendentals=0),
        )(*[pltpu.with_memory_space_constraint(a, m) if m else a for a, m in zip(args, spaces)])

    shape = lambda *dims, dtype=F32: jax.ShapeDtypeStruct(dims, dtype)
    lines = lambda count, head=0: shape(count * B + head, B)
    sems = lambda count: pltpu.SemaphoreType.DMA((count,))
    far = lambda a: pltpu.with_memory_space_constraint(a, pltpu.HBM)
    vmem = lambda *dims, dtype=F32: pltpu.VMEM(dims, dtype)
    crossing = lambda r: r - 1 if r % 2 == 0 else r + 1
    cross = lambda r, c: (crossing(r), c)
    twin = lambda r, c: (r ^ 1, c)
    east = lambda r, c: (r, c + 1)
    west = lambda r, c: (r, c - 1)

    messages = call(
        pack_kernel,
        [(lines(12, HEAD), ANY), (lines(6, HEAD), VMEM), (lines(24, HEAD), VMEM), (lines(12), ANY), (lines(6), ANY)],
        (x, pat),
        [ANY, ANY],
        10,
        [vmem(4, 9, B, B), vmem(12 * B + HEAD, B), vmem(6 * B, B), pltpu.SMEM(pat.shape, jnp.int32), sems(17)],
    )
    c1, ea, tw, c2, we = [moved(m, s) for m, s in zip(messages, [cross, east, twin, cross, west])]
    c1m, _, twm = messages[:3]
    acc, lefts, pairs, few = call(
        near_kernel,
        [(shape(36, B, B), ANY), (shape(32, B, B, dtype=BF16), ANY), (shape(B, B), VMEM), (lines(9, 2 * HEAD), VMEM)],
        (alpha, beta, far(c1m), twm, tw),
        [SMEM, SMEM] + [VMEM] * 3,
        14,
        [vmem(36, B, B)] + [vmem(n, B, B, dtype=BF16) for n in (32, 24, 24, 24, 24, 36, 36)] + [sems(5)],
    )
    *corners, shares = call(
        middle_kernel,
        [(lines(8), VMEM), (lines(8), VMEM), (shape(B, B), ANY)],
        (beta, pairs, few, c1, ea, we),
        [SMEM] + [VMEM] * 5,
        4,
        [vmem(B, B), pltpu.SemaphoreType.DMA(())],
    )
    cc, tc = moved(corners[0], cross), moved(corners[1], twin)
    gathered = lax.all_to_all(shares, AXES, 0, 0)
    (updated,) = call(
        final_kernel,
        [(shape(*x.shape), ANY)],
        (pat, far(lefts), far(acc), c1, far(c2), *corners, cc, tc),
        [SMEM] + [VMEM] * 8,
        14,
        [vmem(36, B, B), vmem(4, 9, B, B), sems(4)],
    )
    scale = 1.0 / (rows * columns * x.shape[1])
    (trace,) = call(functools.partial(sum_kernel, scale), [(shape(1, 1), SMEM)], (gathered, updated), [VMEM, ANY], 2)
    return (updated, trace.reshape(()))


def solution(mesh):
    placed = (P("row", "col", None, None, None), P("row", "col", None), P(), P())
    return jax.shard_map(
        body,
        mesh=mesh,
        in_specs=placed,
        out_specs=(P("row", "col", None, None, None), P()),
        check_vma=False,
    )
```

```python
import functools

import jax
import jax.numpy as jnp
from jax import lax
from jax.experimental import pallas as pl
from jax.experimental.pallas import tpu as pltpu
from jax.sharding import PartitionSpec as P

CR, TW, MID = KINDS = (0, 1, 2)
AXES = ("row", "col")
B = 128
F32 = jnp.float32
BF16 = jnp.bfloat16
ANY = pl.BlockSpec(memory_space=pl.ANY)
VMEM = pl.BlockSpec(memory_space=pltpu.VMEM)
FAR = None
SMEM = pl.BlockSpec(memory_space=pltpu.SMEM)


def at(kind, v, j):
    return kind * 12 + v * 3 + j + 1


SIDE = {CR: 0, MID: 2, TW: 4}
HEAD = 8


def slot(kind, dv, odd):
    base = {CR: 6 * odd, MID: 3, TW: 6 - 6 * odd}[kind]
    return base + dv + 1


def weight(pat, v, s):
    return pat[0, v, s].astype(F32)


def split(block):
    high = block.astype(BF16)
    return high, (block - high.astype(F32)).astype(BF16)


def dot3(left, right):
    def side(blocks, part):
        return jnp.concatenate([jnp.concatenate([b[part] for b in line], axis=1) for line in blocks], axis=0)

    lh, ll, rh, rl = side(left, 0), side(left, 1), side(right, 0), side(right, 1)
    return jnp.dot(
        jnp.concatenate([lh, lh, ll], axis=1), jnp.concatenate([rh, rl, rh], axis=0), preferred_element_type=F32
    )


def get(ref, i, head=0):
    return ref[pl.ds(head + i * B, B), :]


def put(ref, i, block, head=0):
    ref[pl.ds(head + i * B, B), :] = block


class Copies:
    def __init__(self, sems):
        self.sems, self.count = sems, 0

    def start(self, source, target):
        copy = pltpu.make_async_copy(source, target, self.sems.at[self.count])
        self.count += 1
        copy.start()
        return copy


def pack_kernel(x, pat, c1, ea, tw, c2, we, stage, toward, westward, table, sems):
    odd = lax.rem(lax.axis_index("row"), 2)
    dma = Copies(sems)
    table_load = dma.start(pat, table)
    order = [(CR, v) for v in (0, 3, 1, 2)] + [(k, v) for v in (0, 3) for k in (MID, TW)] + [(k, v) for k in (MID, TW) for v in (1, 2)]
    loads = {}
    for kind, v in order:
        slots = pl.ds(slot(kind, -1, odd), 3)
        loads[kind, v] = dma.start(x.at[0, v, slots], stage.at[v, slots])
    table_load.wait()
    rows = lax.broadcasted_iota(jnp.int32, (HEAD, B), 0)
    present = jnp.zeros((HEAD, B), F32)
    for v in range(4):
        present = jnp.where(rows == v, weight(table, v, 4), present)
    for ref in (toward, ea, tw):
        ref[pl.ds(0, HEAD), :] = present

    stores = []
    for kind, v in order:
        loads[kind, v].wait()
        for j in (-1, 0, 1):
            s = slot(kind, j, odd)
            block = stage[v, s] * weight(table, v, s)
            i = at(kind, v, j)
            if kind == CR:
                put(toward, i, block, HEAD)
            else:
                put(tw, i - 12, block, HEAD)
            if v == 3 and j >= 0:
                put(ea, SIDE[kind] + j, block, HEAD)
            if v == 0 and j < 1:
                put(westward, SIDE[kind] + j + 1, block)
        if (kind, v) == (CR, 2):
            stores.append(dma.start(toward, c1))
        if (kind, v) == (MID, 2):
            stores.append(dma.start(tw.at[pl.ds(HEAD + 12 * B, 12 * B), :], c2))
        if v == 0 and all((k, 0) in order[: order.index((kind, v)) + 1] for k in KINDS):
            stores.append(dma.start(westward, we))
    for copy in stores:
        copy.wait()


def near_kernel(alpha, beta, c1m, twm, tw, acc, lefts, pairs, few, total, lefts_here, lh, ll, sh, sl, rh, rl, sems):
    dma = Copies(sems)
    stores = []
    def own(kind, v, j):
        i = at(kind, v, j)
        return get(c1m, i, HEAD) if kind == CR else get(twm, i - 12, HEAD)

    sources = {at(CR, v, a): at(CR, v, a) for v in range(4) for a in (-1, 0, 1)}
    sources.update({at(TW, 0, -1): 12, at(TW, 3, 1): 13, at(MID, 0, -1): 14, at(MID, 3, 1): 15})

    def prepare(v):
        for kind in KINDS:
            for j in (-1, 0, 1):
                i = at(kind, v, j)
                block = own(kind, v, j)
                total[v * 9 + kind * 3 + j + 1] = alpha[()] * block
                rh[i], rl[i] = split(block)
                high, low = split(beta[()] * block)
                if kind != CR:
                    lh[i - 12], ll[i - 12] = high, low
                if i in sources:
                    lefts_here[sources[i]], lefts_here[16 + sources[i]] = high, low
        for j in (-1, 0, 1):
            for kind in (TW, MID):
                i = at(kind, v, j) - 12
                sh[i], sl[i] = split(get(tw, i, HEAD))

    left = lambda kind, v, j: (lh[at(kind, v, j) - 12], ll[at(kind, v, j) - 12])
    mine = lambda kind, v, j: (rh[at(kind, v, j)], rl[at(kind, v, j)])
    theirs = lambda kind, v, j: (sh[at(kind, v, j) - 12], sl[at(kind, v, j) - 12])

    def add(kind, v, sv, block):
        total[v * 9 + kind * 3 + sv + 1] += block

    for w in range(4):
        prepare(w)
    stores.append(dma.start(lefts_here, lefts))
    for w in range(4):
        for t in (0, -1, 1):
            targets = [(w - a, a) for a in (-1, 0, 1) if 0 <= w - a < 4 and -1 <= a + t <= 1]
            lines = [[left(MID, v, a), left(TW, v, a)] for v, a in targets]
            right = [[mine(MID, w, t), mine(TW, w, t)], [theirs(TW, w, t), theirs(MID, w, t)]]
            both = dot3(lines, right)
            only = dot3([line[:1] for line in lines], [[mine(CR, w, t)]])
            for n, (v, a) in enumerate(targets):
                rows = slice(n * B, (n + 1) * B)
                add(MID, v, a + t, both[rows, :B])
                add(TW, v, a + t, both[rows, B:])
                add(CR, v, a + t, only[rows])
        for v in range(4):
            if w == min(v + 1, 3):
                stores.append(dma.start(total.at[pl.ds(v * 9, 9)], acc.at[pl.ds(v * 9, 9)]))
    present = lambda v: twm[pl.ds(v, 1), :]
    other = lambda v: tw[pl.ds(v, 1), :]
    listed = []
    for v in range(4):
        listed.append((own(MID, v, 0), mine(MID, v, 0)))
        listed.append((own(TW, v, 0) * present(v), theirs(TW, v, 0)))
    for v in range(3):
        listed.append((own(MID, v, 1) * (present(v) + present(v + 1)), mine(MID, v + 1, -1)))
        listed.append((own(TW, v + 1, -1) * (present(v + 1) + other(v)), theirs(TW, v, 1)))
    value = beta[()] * dot3([[split(a) for a, _ in listed]], [[b] for _, b in listed])
    for v in range(4):
        value += alpha[()] * own(MID, v, 0)
    pairs[...] = value
    few[pl.ds(0, HEAD), :] = twm[pl.ds(0, HEAD), :]
    few[pl.ds(HEAD, HEAD), :] = tw[pl.ds(0, HEAD), :]
    kept = [own(CR, v, 0) for v in range(4)] + [own(CR, v, -1) for v in (1, 2, 3)] + [own(MID, 0, -1), get(tw, 0, HEAD)]
    for i, block in enumerate(kept):
        put(few, i, block, 2 * HEAD)
    for copy in stores:
        copy.wait()


def middle_kernel(beta, pairs, few, c1, ea, we, cc, tc, shares, lines, sem):
    own = lambda v: few[pl.ds(v, 1), :]
    far = lambda v: c1[pl.ds(v, 1), :]
    west = ea[pl.ds(3, 1), :]
    kept = lambda i: get(few, i, 2 * HEAD)
    listed = []
    for v in range(4):
        listed.append((own(v), kept(v), get(c1, at(CR, v, 0), HEAD)))
    for v in range(3):
        listed.append((own(v + 1) + far(v), kept(4 + v), get(c1, at(CR, v, 1), HEAD)))
    listed.append((west + own(0), get(ea, SIDE[MID] + 1, HEAD), kept(7)))
    listed.append((west + far(0), get(ea, SIDE[CR] + 1, HEAD), get(c1, 0, HEAD)))
    listed.append((west + few[pl.ds(HEAD, 1), :], get(ea, SIDE[TW] + 1, HEAD), kept(8)))
    value = pairs[...] + beta[()] * dot3([[split(a * w) for w, a, _ in listed]], [[split(b)] for _, _, b in listed])
    rows = lax.broadcasted_iota(jnp.int32, (B, B), 0)
    columns = lax.broadcasted_iota(jnp.int32, (B, B), 1)
    line = jnp.sum(jnp.where(rows == columns, value, 0.0), axis=0, keepdims=True)
    lines[...] = jnp.broadcast_to(line, (B, B))
    copy = pltpu.make_async_copy(lines, shares, sem)
    copy.start()
    for out, kind in ((cc, CR), (tc, MID)):
        for i in range(4):
            put(out, i, get(ea, SIDE[kind] + i, HEAD))
            put(out, 4 + i, get(we, SIDE[kind] + i))
    copy.wait()


def sum_kernel(scale, shares, after, out):
    out[0, 0] = jnp.sum(shares[...]) * scale


def final_kernel(pat, lefts, acc, c1, c2, ccm, tcm, cc, tc, out, total, stage, sems):
    odd = lax.rem(lax.axis_index("row"), 2)
    dma = Copies(sems)
    left = lambda i: (lefts[i], lefts[16 + i])
    seen = set()

    def add(kind, v, sv, block):
        i = v * 9 + kind * 3 + sv + 1
        total[i] = (total[i] if i in seen else acc[i]) + block
        seen.add(i)

    def spread(source, rights, places):
        result = dot3([[left(source)]], [[split(block) for block in rights]])
        for n, (kind, v, sv) in enumerate(places):
            add(kind, v, sv, result[:, n * B : (n + 1) * B])

    spread(14, [get(ccm, i) for i in range(4)] + [get(tcm, i) for i in (2, 3)], [(k, 0, s) for k in SIDE for s in (-1, 0)])
    spread(15, [get(ccm, 4 + i) for i in range(4)] + [get(tcm, i) for i in (6, 7)], [(k, 3, s) for k in SIDE for s in (0, 1)])
    spread(12, [get(tc, i) for i in range(4)], [(TW, 0, -1), (TW, 0, 0), (MID, 0, -1), (MID, 0, 0)])
    spread(13, [get(tc, 4 + i) for i in range(4)], [(TW, 3, 0), (TW, 3, 1), (MID, 3, 0), (MID, 3, 1)])
    spread(at(CR, 0, -1), [get(cc, i) for i in range(4)], [(MID, 0, -1), (MID, 0, 0), (CR, 0, -1), (CR, 0, 0)])
    spread(at(CR, 3, 1), [get(cc, 4 + i) for i in range(4)], [(MID, 3, 0), (MID, 3, 1), (CR, 3, 0), (CR, 3, 1)])

    stores = []

    def finish(v):
        for kind in KINDS:
            for sv in (-1, 0, 1):
                i, s = v * 9 + kind * 3 + sv + 1, slot(kind, sv, odd)
                stage[v, s] = weight(pat, v, s) * (total[i] if i in seen else acc[i])
        stores.append(dma.start(stage.at[v], out.at[0, v]))

    for w in range(4):
        for t in (0, -1, 1):
            targets = [(w - a, a) for a in (-1, 0, 1) if 0 <= w - a < 4 and -1 <= a + t <= 1]
            lines = [[left(at(CR, v, a))] for v, a in targets]
            result = dot3(lines, [[split(get(c1, at(CR, w, t), HEAD)), split(get(c2, at(CR, w, t)))]])
            for n, (v, a) in enumerate(targets):
                rows = slice(n * B, (n + 1) * B)
                add(MID, v, a + t, result[rows, :B])
                add(CR, v, a + t, result[rows, B:])
        if w >= 1:
            finish(w - 1)
    finish(3)
    for copy in stores:
        copy.wait()


def body(x, pat, alpha, beta):
    rows, columns = lax.axis_size("row"), lax.axis_size("col")

    def moved(message, step):
        pairs = []
        for r in range(rows):
            for c in range(columns):
                r2, c2 = step(r, c)
                pairs.append((r * columns + c, (r2 % rows) * columns + c2 % columns))
        return lax.ppermute(message, AXES, pairs)

    def call(kernel, outs, args, specs, size, scratch=()):
        spaces = [pltpu.HBM if s is ANY or a is pat else None for a, s in zip(args, specs)]
        return pl.pallas_call(
            kernel,
            out_shape=[pltpu.HBM(o.shape, o.dtype) if s is ANY or s is FAR else o for o, s in outs],
            in_specs=specs,
            out_specs=[VMEM if s is FAR else s for _, s in outs],
            scratch_shapes=scratch,
            compiler_params=pltpu.CompilerParams(vmem_limit_bytes=size * 1024 * 1024),
            cost_estimate=pl.CostEstimate(flops=1000, bytes_accessed=1000, transcendentals=0),
        )(*[pltpu.with_memory_space_constraint(a, m) if m else a for a, m in zip(args, spaces)])

    shape = lambda *dims, dtype=F32: jax.ShapeDtypeStruct(dims, dtype)
    lines = lambda count, head=0: shape(count * B + head, B)
    sems = lambda count: pltpu.SemaphoreType.DMA((count,))
    far = lambda a: pltpu.with_memory_space_constraint(a, pltpu.HBM)
    vmem = lambda *dims, dtype=F32: pltpu.VMEM(dims, dtype)
    crossing = lambda r: r - 1 if r % 2 == 0 else r + 1
    cross = lambda r, c: (crossing(r), c)
    twin = lambda r, c: (r ^ 1, c)
    east = lambda r, c: (r, c + 1)
    west = lambda r, c: (r, c - 1)

    messages = call(
        pack_kernel,
        [(lines(12, HEAD), ANY), (lines(6, HEAD), VMEM), (lines(24, HEAD), VMEM), (lines(12), ANY), (lines(6), ANY)],
        (x, pat),
        [ANY, ANY],
        10,
        [vmem(4, 9, B, B), vmem(12 * B + HEAD, B), vmem(6 * B, B), pltpu.SMEM(pat.shape, jnp.int32), sems(17)],
    )
    c1, ea, tw, c2, we = [moved(m, s) for m, s in zip(messages, [cross, east, twin, cross, west])]
    c1m, _, twm = messages[:3]
    acc, lefts, pairs, few = call(
        near_kernel,
        [(shape(36, B, B), ANY), (shape(32, B, B, dtype=BF16), ANY), (shape(B, B), VMEM), (lines(9, 2 * HEAD), VMEM)],
        (alpha, beta, far(c1m), twm, tw),
        [SMEM, SMEM] + [VMEM] * 3,
        14,
        [vmem(36, B, B)] + [vmem(n, B, B, dtype=BF16) for n in (32, 24, 24, 24, 24, 36, 36)] + [sems(5)],
    )
    *corners, shares = call(
        middle_kernel,
        [(lines(8), VMEM), (lines(8), VMEM), (shape(B, B), ANY)],
        (beta, pairs, few, c1, ea, we),
        [SMEM] + [VMEM] * 5,
        4,
        [vmem(B, B), pltpu.SemaphoreType.DMA(())],
    )
    cc, tc = moved(corners[0], cross), moved(corners[1], twin)
    gathered = lax.all_to_all(shares, AXES, 0, 0)
    (updated,) = call(
        final_kernel,
        [(shape(*x.shape), ANY)],
        (pat, far(lefts), far(acc), c1, far(c2), *corners, cc, tc),
        [SMEM] + [VMEM] * 8,
        14,
        [vmem(36, B, B), vmem(4, 9, B, B), sems(4)],
    )
    scale = 1.0 / (rows * columns * x.shape[1])
    (trace,) = call(functools.partial(sum_kernel, scale), [(shape(1, 1), SMEM)], (gathered, updated), [VMEM, ANY], 2)
    return (updated, trace.reshape(()))


def solution(mesh):
    placed = (P("row", "col", None, None, None), P("row", "col", None), P(), P())
    return jax.shard_map(
        body,
        mesh=mesh,
        in_specs=placed,
        out_specs=(P("row", "col", None, None, None), P()),
        check_vma=False,
    )
```

```python
import functools

import jax
import jax.numpy as jnp
from jax import lax
from jax.experimental import pallas as pl
from jax.experimental.pallas import tpu as pltpu
from jax.sharding import PartitionSpec as P

CR, TW, MID = KINDS = (0, 1, 2)
AXES = ("row", "col")
B = 128
F32 = jnp.float32
BF16 = jnp.bfloat16
ANY = pl.BlockSpec(memory_space=pl.ANY)
VMEM = pl.BlockSpec(memory_space=pltpu.VMEM)
FAR = None
SMEM = pl.BlockSpec(memory_space=pltpu.SMEM)


def at(kind, v, j):
    return kind * 12 + v * 3 + j + 1


SIDE = {CR: 0, MID: 2, TW: 4}
HEAD = 8


def slot(kind, dv, odd):
    base = {CR: 6 * odd, MID: 3, TW: 6 - 6 * odd}[kind]
    return base + dv + 1


def weight(pat, v, s):
    return pat[0, v, s].astype(F32)


def split(block):
    high = block.astype(BF16)
    return high, (block - high.astype(F32)).astype(BF16)


def dot3(left, right):
    def side(blocks, part):
        return jnp.concatenate([jnp.concatenate([b[part] for b in line], axis=1) for line in blocks], axis=0)

    lh, ll, rh, rl = side(left, 0), side(left, 1), side(right, 0), side(right, 1)
    return jnp.dot(
        jnp.concatenate([lh, lh, ll], axis=1), jnp.concatenate([rh, rl, rh], axis=0), preferred_element_type=F32
    )


def get(ref, i, head=0):
    return ref[pl.ds(head + i * B, B), :]


def put(ref, i, block, head=0):
    ref[pl.ds(head + i * B, B), :] = block


class Copies:
    def __init__(self, sems):
        self.sems, self.count = sems, 0

    def start(self, source, target):
        copy = pltpu.make_async_copy(source, target, self.sems.at[self.count])
        self.count += 1
        copy.start()
        return copy


def pack_kernel(x, pat, c1, ea, tw, c2, we, stage, toward, westward, table, sems):
    odd = lax.rem(lax.axis_index("row"), 2)
    dma = Copies(sems)
    table_load = dma.start(pat, table)
    order = [(CR, v) for v in (0, 3, 1, 2)] + [(MID, 0), (TW, 0)] + [(MID, v) for v in (3, 1, 2)] + [(TW, v) for v in (3, 1, 2)]
    loads = {}
    for kind, v in order:
        slots = pl.ds(slot(kind, -1, odd), 3)
        loads[kind, v] = dma.start(x.at[0, v, slots], stage.at[v, slots])
    table_load.wait()
    rows = lax.broadcasted_iota(jnp.int32, (HEAD, B), 0)
    present = jnp.zeros((HEAD, B), F32)
    for v in range(4):
        present = jnp.where(rows == v, weight(table, v, 4), present)
    for ref in (toward, ea, tw):
        ref[pl.ds(0, HEAD), :] = present

    stores = []
    for kind, v in order:
        loads[kind, v].wait()
        for j in (-1, 0, 1):
            s = slot(kind, j, odd)
            block = stage[v, s] * weight(table, v, s)
            i = at(kind, v, j)
            if kind == CR:
                put(toward, i, block, HEAD)
            else:
                put(tw, i - 12, block, HEAD)
            if v == 3 and j >= 0:
                put(ea, SIDE[kind] + j, block, HEAD)
            if v == 0 and j < 1:
                put(westward, SIDE[kind] + j + 1, block)
        if (kind, v) == (CR, 2):
            stores.append(dma.start(toward, c1))
        if (kind, v) == (MID, 2):
            stores.append(dma.start(tw.at[pl.ds(HEAD + 12 * B, 12 * B), :], c2))
        if v == 0 and all((k, 0) in order[: order.index((kind, v)) + 1] for k in KINDS):
            stores.append(dma.start(westward, we))
    for copy in stores:
        copy.wait()


def near_kernel(alpha, beta, c1m, twm, tw, acc, lefts, pairs, few, total, lefts_here, lh, ll, sh, sl, rh, rl, sems):
    dma = Copies(sems)
    stores = []
    def own(kind, v, j):
        i = at(kind, v, j)
        return get(c1m, i, HEAD) if kind == CR else get(twm, i - 12, HEAD)

    sources = {at(CR, v, a): at(CR, v, a) for v in range(4) for a in (-1, 0, 1)}
    sources.update({at(TW, 0, -1): 12, at(TW, 3, 1): 13, at(MID, 0, -1): 14, at(MID, 3, 1): 15})

    def prepare(v):
        for kind in KINDS:
            for j in (-1, 0, 1):
                i = at(kind, v, j)
                block = own(kind, v, j)
                total[v * 9 + kind * 3 + j + 1] = alpha[()] * block
                rh[i], rl[i] = split(block)
                high, low = split(beta[()] * block)
                if kind != CR:
                    lh[i - 12], ll[i - 12] = high, low
                if i in sources:
                    lefts_here[sources[i]], lefts_here[16 + sources[i]] = high, low
        for j in (-1, 0, 1):
            for kind in (TW, MID):
                i = at(kind, v, j) - 12
                sh[i], sl[i] = split(get(tw, i, HEAD))

    left = lambda kind, v, j: (lh[at(kind, v, j) - 12], ll[at(kind, v, j) - 12])
    mine = lambda kind, v, j: (rh[at(kind, v, j)], rl[at(kind, v, j)])
    theirs = lambda kind, v, j: (sh[at(kind, v, j) - 12], sl[at(kind, v, j) - 12])

    def add(kind, v, sv, block):
        total[v * 9 + kind * 3 + sv + 1] += block

    for w in range(4):
        prepare(w)
    stores.append(dma.start(lefts_here, lefts))
    for w in range(4):
        for t in (0, -1, 1):
            targets = [(w - a, a) for a in (-1, 0, 1) if 0 <= w - a < 4 and -1 <= a + t <= 1]
            lines = [[left(MID, v, a), left(TW, v, a)] for v, a in targets]
            right = [[mine(MID, w, t), mine(TW, w, t)], [theirs(TW, w, t), theirs(MID, w, t)]]
            both = dot3(lines, right)
            only = dot3([line[:1] for line in lines], [[mine(CR, w, t)]])
            for n, (v, a) in enumerate(targets):
                rows = slice(n * B, (n + 1) * B)
                add(MID, v, a + t, both[rows, :B])
                add(TW, v, a + t, both[rows, B:])
                add(CR, v, a + t, only[rows])
        for v in range(4):
            if w == min(v + 1, 3):
                stores.append(dma.start(total.at[pl.ds(v * 9, 9)], acc.at[pl.ds(v * 9, 9)]))
    present = lambda v: twm[pl.ds(v, 1), :]
    other = lambda v: tw[pl.ds(v, 1), :]
    listed = []
    for v in range(4):
        listed.append((own(MID, v, 0), mine(MID, v, 0)))
        listed.append((own(TW, v, 0) * present(v), theirs(TW, v, 0)))
    for v in range(3):
        listed.append((own(MID, v, 1) * (present(v) + present(v + 1)), mine(MID, v + 1, -1)))
        listed.append((own(TW, v + 1, -1) * (present(v + 1) + other(v)), theirs(TW, v, 1)))
    value = beta[()] * dot3([[split(a) for a, _ in listed]], [[b] for _, b in listed])
    for v in range(4):
        value += alpha[()] * own(MID, v, 0)
    pairs[...] = value
    few[pl.ds(0, HEAD), :] = twm[pl.ds(0, HEAD), :]
    few[pl.ds(HEAD, HEAD), :] = tw[pl.ds(0, HEAD), :]
    kept = [own(CR, v, 0) for v in range(4)] + [own(CR, v, -1) for v in (1, 2, 3)] + [own(MID, 0, -1), get(tw, 0, HEAD)]
    for i, block in enumerate(kept):
        put(few, i, block, 2 * HEAD)
    for copy in stores:
        copy.wait()


def middle_kernel(beta, pairs, few, c1, ea, we, cc, tc, shares, lines, sem):
    own = lambda v: few[pl.ds(v, 1), :]
    far = lambda v: c1[pl.ds(v, 1), :]
    west = ea[pl.ds(3, 1), :]
    kept = lambda i: get(few, i, 2 * HEAD)
    listed = []
    for v in range(4):
        listed.append((own(v), kept(v), get(c1, at(CR, v, 0), HEAD)))
    for v in range(3):
        listed.append((own(v + 1) + far(v), kept(4 + v), get(c1, at(CR, v, 1), HEAD)))
    listed.append((west + own(0), get(ea, SIDE[MID] + 1, HEAD), kept(7)))
    listed.append((west + far(0), get(ea, SIDE[CR] + 1, HEAD), get(c1, 0, HEAD)))
    listed.append((west + few[pl.ds(HEAD, 1), :], get(ea, SIDE[TW] + 1, HEAD), kept(8)))
    value = pairs[...] + beta[()] * dot3([[split(a * w) for w, a, _ in listed]], [[split(b)] for _, _, b in listed])
    rows = lax.broadcasted_iota(jnp.int32, (B, B), 0)
    columns = lax.broadcasted_iota(jnp.int32, (B, B), 1)
    line = jnp.sum(jnp.where(rows == columns, value, 0.0), axis=0, keepdims=True)
    lines[...] = jnp.broadcast_to(line, (B, B))
    copy = pltpu.make_async_copy(lines, shares, sem)
    copy.start()
    for out, kind in ((cc, CR), (tc, MID)):
        for i in range(4):
            put(out, i, get(ea, SIDE[kind] + i, HEAD))
            put(out, 4 + i, get(we, SIDE[kind] + i))
    copy.wait()


def sum_kernel(scale, shares, after, out):
    out[0, 0] = jnp.sum(shares[...]) * scale


def final_kernel(pat, lefts, acc, c1, c2, ccm, tcm, cc, tc, out, total, stage, sems):
    odd = lax.rem(lax.axis_index("row"), 2)
    dma = Copies(sems)
    left = lambda i: (lefts[i], lefts[16 + i])
    seen = set()

    def add(kind, v, sv, block):
        i = v * 9 + kind * 3 + sv + 1
        total[i] = (total[i] if i in seen else acc[i]) + block
        seen.add(i)

    def spread(source, rights, places):
        result = dot3([[left(source)]], [[split(block) for block in rights]])
        for n, (kind, v, sv) in enumerate(places):
            add(kind, v, sv, result[:, n * B : (n + 1) * B])

    spread(14, [get(ccm, i) for i in range(4)] + [get(tcm, i) for i in (2, 3)], [(k, 0, s) for k in SIDE for s in (-1, 0)])
    spread(15, [get(ccm, 4 + i) for i in range(4)] + [get(tcm, i) for i in (6, 7)], [(k, 3, s) for k in SIDE for s in (0, 1)])
    spread(12, [get(tc, i) for i in range(4)], [(TW, 0, -1), (TW, 0, 0), (MID, 0, -1), (MID, 0, 0)])
    spread(13, [get(tc, 4 + i) for i in range(4)], [(TW, 3, 0), (TW, 3, 1), (MID, 3, 0), (MID, 3, 1)])
    spread(at(CR, 0, -1), [get(cc, i) for i in range(4)], [(MID, 0, -1), (MID, 0, 0), (CR, 0, -1), (CR, 0, 0)])
    spread(at(CR, 3, 1), [get(cc, 4 + i) for i in range(4)], [(MID, 3, 0), (MID, 3, 1), (CR, 3, 0), (CR, 3, 1)])

    stores = []

    def finish(v):
        for kind in KINDS:
            for sv in (-1, 0, 1):
                i, s = v * 9 + kind * 3 + sv + 1, slot(kind, sv, odd)
                stage[v, s] = weight(pat, v, s) * (total[i] if i in seen else acc[i])
        stores.append(dma.start(stage.at[v], out.at[0, v]))

    for w in range(4):
        for t in (0, -1, 1):
            targets = [(w - a, a) for a in (-1, 0, 1) if 0 <= w - a < 4 and -1 <= a + t <= 1]
            lines = [[left(at(CR, v, a))] for v, a in targets]
            result = dot3(lines, [[split(get(c1, at(CR, w, t), HEAD)), split(get(c2, at(CR, w, t)))]])
            for n, (v, a) in enumerate(targets):
                rows = slice(n * B, (n + 1) * B)
                add(MID, v, a + t, result[rows, :B])
                add(CR, v, a + t, result[rows, B:])
        if w >= 1:
            finish(w - 1)
    finish(3)
    for copy in stores:
        copy.wait()


def body(x, pat, alpha, beta):
    rows, columns = lax.axis_size("row"), lax.axis_size("col")

    def moved(message, step):
        pairs = []
        for r in range(rows):
            for c in range(columns):
                r2, c2 = step(r, c)
                pairs.append((r * columns + c, (r2 % rows) * columns + c2 % columns))
        return lax.ppermute(message, AXES, pairs)

    def call(kernel, outs, args, specs, size, scratch=()):
        spaces = [pltpu.HBM if s is ANY or a is pat else None for a, s in zip(args, specs)]
        return pl.pallas_call(
            kernel,
            out_shape=[pltpu.HBM(o.shape, o.dtype) if s is ANY or s is FAR else o for o, s in outs],
            in_specs=specs,
            out_specs=[VMEM if s is FAR else s for _, s in outs],
            scratch_shapes=scratch,
            compiler_params=pltpu.CompilerParams(vmem_limit_bytes=size * 1024 * 1024),
            cost_estimate=pl.CostEstimate(flops=1000, bytes_accessed=1000, transcendentals=0),
        )(*[pltpu.with_memory_space_constraint(a, m) if m else a for a, m in zip(args, spaces)])

    shape = lambda *dims, dtype=F32: jax.ShapeDtypeStruct(dims, dtype)
    lines = lambda count, head=0: shape(count * B + head, B)
    sems = lambda count: pltpu.SemaphoreType.DMA((count,))
    far = lambda a: pltpu.with_memory_space_constraint(a, pltpu.HBM)
    vmem = lambda *dims, dtype=F32: pltpu.VMEM(dims, dtype)
    crossing = lambda r: r - 1 if r % 2 == 0 else r + 1
    cross = lambda r, c: (crossing(r), c)
    twin = lambda r, c: (r ^ 1, c)
    east = lambda r, c: (r, c + 1)
    west = lambda r, c: (r, c - 1)

    messages = call(
        pack_kernel,
        [(lines(12, HEAD), ANY), (lines(6, HEAD), VMEM), (lines(24, HEAD), VMEM), (lines(12), ANY), (lines(6), ANY)],
        (x, pat),
        [ANY, ANY],
        10,
        [vmem(4, 9, B, B), vmem(12 * B + HEAD, B), vmem(6 * B, B), pltpu.SMEM(pat.shape, jnp.int32), sems(17)],
    )
    c1, ea, tw, c2, we = [moved(m, s) for m, s in zip(messages, [cross, east, twin, cross, west])]
    c1m, _, twm = messages[:3]
    acc, lefts, pairs, few = call(
        near_kernel,
        [(shape(36, B, B), ANY), (shape(32, B, B, dtype=BF16), ANY), (shape(B, B), VMEM), (lines(9, 2 * HEAD), VMEM)],
        (alpha, beta, far(c1m), twm, tw),
        [SMEM, SMEM] + [VMEM] * 3,
        14,
        [vmem(36, B, B)] + [vmem(n, B, B, dtype=BF16) for n in (32, 24, 24, 24, 24, 36, 36)] + [sems(5)],
    )
    *corners, shares = call(
        middle_kernel,
        [(lines(8), VMEM), (lines(8), VMEM), (shape(B, B), ANY)],
        (beta, pairs, few, c1, ea, we),
        [SMEM] + [VMEM] * 5,
        4,
        [vmem(B, B), pltpu.SemaphoreType.DMA(())],
    )
    cc, tc = moved(corners[0], cross), moved(corners[1], twin)
    gathered = lax.all_to_all(shares, AXES, 0, 0)
    (updated,) = call(
        final_kernel,
        [(shape(*x.shape), ANY)],
        (pat, far(lefts), far(acc), c1, far(c2), *corners, cc, tc),
        [SMEM] + [VMEM] * 8,
        14,
        [vmem(36, B, B), vmem(4, 9, B, B), sems(4)],
    )
    scale = 1.0 / (rows * columns * x.shape[1])
    (trace,) = call(functools.partial(sum_kernel, scale), [(shape(1, 1), SMEM)], (gathered, updated), [VMEM, ANY], 2)
    return (updated, trace.reshape(()))


def solution(mesh):
    placed = (P("row", "col", None, None, None), P("row", "col", None), P(), P())
    return jax.shard_map(
        body,
        mesh=mesh,
        in_specs=placed,
        out_specs=(P("row", "col", None, None, None), P()),
        check_vma=False,
    )
```
